32 devices in a mesh: param: 4 (over y, x), slab: 8 (over z, core).
Axes of the slice: x: 2, y: 2, z: 4, core: 2. Of those that a mesh axis runs over, the one named last changes fastest.
Arguments:
- init_state: float32 [4, 128, 128, 128], P('param', None, 'slab'), may hold values from -6 to 6
- coef: float32 [4, 128, 128], P('param', 'slab'), may hold values from 0.06 to 0.16
- source: float32 [128, 128], P('slab'), may hold values from -6 to 6
- amplitudes: float32 [64], replicated, may hold values from 0.5 to 2
- sample_idx: int32 [4, 128], P('param'), may hold values from 0 to 63
- step_counts: int32 [4], P('param'), may hold values from 1 to 8, as said below
- sketch_signs: int32 [3, 128, 64], replicated, may hold values from 0 to 1
Outputs:
- modes: float32 [64, 128, 128], P(None, 'slab', 'param')
The draws below stay inside these ranges and needn't reach their ends.
Inputs may be any that keep to these rules, and one draw needn't show every extreme that they name: `step_counts`: one group takes all 8 steps and another exactly one.
All inputs are finite; a program needn't handle non-finite values.
Results may differ from the reference program's by a relative error of at most 0.0003.
Values sent between devices are 32-bit elements; how exact they have to be, the bound alone decides.
A program may use at most 64 MiB of HBM per device.

```python
import math
import jax
import jax.numpy as jnp
from jax import lax

S = 128
R = 64
NZ = 128
STEPS = 8
PTAB = 64
GROUPS = 4
NX = 128
LEVELS = 2


def draw_step_counts(key, part):
    first_key, second_key = jax.random.split(jax.random.fold_in(key, 7))
    counts = jax.random.randint(first_key, (GROUPS,), 1, STEPS + 1)
    order = jax.random.permutation(second_key, GROUPS)
    counts = counts.at[order[0]].set(STEPS)
    counts = counts.at[order[1]].set(1)
    return counts.astype(jnp.int32)


def with_ends(entries, stream_key, smallest, top_value):
    extent = entries.shape
    index_at = [jax.random.randint(jax.random.fold_in(stream_key, axis), (), 0, extent[axis]) for axis in range(len(extent))]
    entries = entries.at[tuple(index_at)].set(smallest)
    longest = extent.index(max(extent))
    index_at[longest] = (index_at[longest] + 1) % extent[longest]
    return entries.at[tuple(index_at)].set(top_value)


def shard_levels(key, dims, shards, low, top_value):
    def one(axis_at, blocks):
        steps = jax.random.uniform(jax.random.fold_in(jax.random.fold_in(key, 6), axis_at), (blocks,), jnp.float32, low / len(shards), top_value / len(shards))
        return jnp.repeat(jnp.exp(steps), dims[axis_at] // blocks).reshape((-1,) + (1,) * (len(dims) - axis_at - 1))

    loudness = one(*shards[0])
    for cut in shards[1:]:
        loudness = loudness * one(*cut)
    return loudness


def normal_values(own_key, extent, deviation, bound, cuts=(), held_as=jnp.bfloat16):
    level = shard_levels(own_key, extent, cuts, -0.22, 0.18) if cuts else 1.0
    result = jax.random.normal(own_key, extent, jnp.float32) * deviation * level
    return jnp.minimum(jnp.maximum(result, -bound), bound).astype(held_as)


def setup_inputs(seed: int = 0) -> dict:
    key_list = jax.random.split(jax.random.key(seed), 8)
    return {
        "init_state": normal_values(key_list[0], (GROUPS, S, NX, NZ), 1.0, 6.0, ((0, 4), (2, 8)), jnp.float32),
        "coef": jnp.clip(jnp.exp(math.log(0.16) - 0.98082925 * jax.random.uniform(key_list[1], (GROUPS, NX, NZ), jnp.float32) ** shard_levels(key_list[1], (GROUPS, NX, NZ), ((0, 4), (1, 8)), -0.2, 0.2)), 0.06, 0.16),
        "source": normal_values(key_list[2], (NX, NZ), 1.0, 6.0, ((0, 8),), jnp.float32),
        "amplitudes": jnp.clip(jnp.exp(jax.random.uniform(key_list[3], (PTAB,), jnp.float32, math.log(0.5), math.log(2.0))), 0.5, 2.0),
        "sample_idx": with_ends(jax.random.randint(key_list[4], (GROUPS, S), 0, PTAB), jax.random.fold_in(key_list[4], 1), 0, PTAB - 1).astype(jnp.int32),
        "step_counts": draw_step_counts(jax.random.fold_in(key_list[7], 71), 0),
        "sketch_signs": with_ends(jax.random.randint(key_list[6], (LEVELS + 1, S, R), 0, 2), jax.random.fold_in(key_list[6], 1), 0, 1).astype(jnp.int32),
    }


def omega_rows(sketch_signs, level):
    signs = sketch_signs[level].astype(jnp.float32)
    return (2.0 * signs - 1.0).T / math.sqrt(sketch_signs.shape[1])

def compress(stacked, gram, omega_t):
    highest = lax.Precision.HIGHEST
    modes_kept = omega_t.shape[0]
    ident = jnp.eye(modes_kept, dtype=jnp.float32)
    moment = jnp.dot(jnp.dot(omega_t, gram, precision=highest), omega_t.T, precision=highest)
    moment = moment + 0.0001 * jnp.trace(moment) / modes_kept * ident
    lower = jnp.linalg.cholesky(moment)
    left = jax.scipy.linalg.solve_triangular(lower, omega_t, lower=True)
    hmat = jnp.dot(left, gram, precision=highest)
    inner = jnp.dot(hmat, hmat.T, precision=highest)
    inner = inner + 0.0001 * jnp.trace(inner) / modes_kept * ident
    factor = jnp.linalg.cholesky(inner)
    mixing = jnp.dot(factor.T, left, precision=highest)
    return jnp.dot(mixing, stacked, precision=highest)

def reference(init_state, coef, source, amplitudes, sample_idx, step_counts, sketch_signs):
    highest = lax.Precision.HIGHEST

    def leaf(inputs):
        field, rate_base, picks, count = inputs
        amp = amplitudes[picks]
        forcing = 0.1 * amp[:, None, None] * source[None]
        for step in range(STEPS):
            padded = jnp.pad(field, ((0, 0), (1, 1), (1, 1)))
            lap = padded[:, 2:, 1:-1] + padded[:, :-2, 1:-1] + padded[:, 1:-1, 2:] + padded[:, 1:-1, :-2] - 4.0 * field
            new = field + rate_base * (1.0 + 0.5 * jnp.tanh(field) ** 2) * lap + forcing
            field = jnp.where(step < count, new, field)
        stacked = field.reshape(field.shape[0], -1)
        gram = jnp.dot(stacked, stacked.T, precision=highest)
        return compress(stacked, gram, omega_rows(sketch_signs, 0))
    pieces = lax.map(leaf, (init_state, coef, sample_idx, step_counts))
    scale_half = 0.5 ** 0.5
    for level in range(LEVELS):
        paired = pieces.reshape(pieces.shape[0] // 2, 2 * pieces.shape[1], pieces.shape[2])
        omega_t = omega_rows(sketch_signs, level + 1)

        def merge(stacked):
            stacked = stacked * scale_half
            gram = jnp.dot(stacked, stacked.T, precision=highest)
            return compress(stacked, gram, omega_t)
        pieces = lax.map(merge, paired)
    return pieces[0].reshape(pieces.shape[1], NX, NZ)
```

```python
import functools
import math

import jax
import jax.numpy as jnp
from jax import lax
from jax.experimental import pallas as pl
from jax.experimental.pallas import tpu as pltpu
from jax.sharding import PartitionSpec as P

STEPS = 8
MESH = pl.DeviceIdType.MESH
HIGHEST = lax.Precision.HIGHEST
VMEM_LIMIT = 48 * 1024 * 1024
VMEM = pl.BlockSpec(memory_space=pltpu.VMEM)
SMEM = pl.BlockSpec(memory_space=pltpu.SMEM)


def dot(a, b):
    return lax.dot_general(a, b, (((1,), (0,)), ((), ())), precision=HIGHEST, preferred_element_type=jnp.float32)


def dot_t(a, b):
    return lax.dot_general(a, b, (((1,), (1,)), ((), ())), precision=HIGHEST, preferred_element_type=jnp.float32)


def flow_kernel(slabs, x_ref, coef_ref, source_ref, table_ref, idx_ref, count_ref, field_ref, gram_ref,
                buf, halo, amp_ref, part, pieces, total, halo_send, halo_recv, rs_send, rs_recv, ag_send, ag_recv):
    rows, cols = coef_ref.shape
    snaps = gram_ref.shape[0]
    share = snaps // slabs
    me = lax.axis_index("slab")
    place = lax.axis_index("param")
    peers = [lax.rem(me + k, slabs) for k in range(1, slabs)]

    barrier = pltpu.get_barrier_semaphore()
    for peer in peers:
        pl.semaphore_signal(barrier, inc=1, device_id=(place, peer), device_id_type=MESH)

    for r in range(rows):
        buf[0, r] = x_ref[pl.ds(r, snaps, stride=rows), :]

    table = jnp.broadcast_to(table_ref[...], (8, table_ref.shape[1]))
    entry = lax.broadcasted_iota(jnp.int32, (table_ref.shape[1], snaps), 0)
    picks = jnp.where(entry == idx_ref[...], 1.0, 0.0)
    amp_row = 0.1 * dot(table, picks)[0:1]
    amp_ref[...] = jnp.transpose(jnp.broadcast_to(amp_row, (cols, snaps)))

    @pl.when(me == 0)
    def _():
        for step in range(STEPS):
            halo[step, 0] = jnp.zeros((snaps, cols), jnp.float32)

    @pl.when(me == slabs - 1)
    def _():
        for step in range(STEPS):
            halo[step, 1] = jnp.zeros((snaps, cols), jnp.float32)

    pl.semaphore_wait(barrier, slabs - 1)

    def down(step):
        return pltpu.make_async_remote_copy(
            src_ref=buf.at[step % 2, rows - 1], dst_ref=halo.at[step, 0],
            send_sem=halo_send.at[step, 0], recv_sem=halo_recv.at[step, 0],
            device_id=(place, lax.rem(me + 1, slabs)), device_id_type=MESH)

    def up(step):
        return pltpu.make_async_remote_copy(
            src_ref=buf.at[step % 2, 0], dst_ref=halo.at[step, 1],
            send_sem=halo_send.at[step, 1], recv_sem=halo_recv.at[step, 1],
            device_id=(place, lax.rem(me + slabs - 1, slabs)), device_id_type=MESH)

    def send(step):
        @pl.when(me < slabs - 1)
        def _():
            down(step).start()

        @pl.when(me > 0)
        def _():
            up(step).start()

    count = count_ref[0]
    chunk = 32
    lane = lax.broadcasted_iota(jnp.int32, (chunk, cols), 1)
    first, last = lane == 0, lane == cols - 1

    def update(step, r, above, below):
        now, later = step % 2, (step + 1) % 2
        active = jnp.where(step < count, 1.0, 0.0)
        rate = coef_ref[pl.ds(r, 1), :] * active
        force = source_ref[pl.ds(r, 1), :] * active
        for c in range(0, snaps, chunk):
            part_rows = pl.ds(c, chunk)
            f = buf[now, r, part_rows]
            left = jnp.where(first, 0.0, pltpu.roll(f, 1, 1))
            right = jnp.where(last, 0.0, pltpu.roll(f, cols - 1, 1))
            lap = below(part_rows) + above(part_rows) + right + left - 4.0 * f
            th = jnp.tanh(f)
            new = f + rate * (1.0 + 0.5 * (th * th)) * lap + amp_ref[part_rows] * force
            buf[later, r, part_rows] = new

    send(0)
    for step in range(STEPS):
        now = step % 2

        def inner(r, carry):
            update(step, r, lambda s: buf[now, r - 1, s], lambda s: buf[now, r + 1, s])
            return carry

        lax.fori_loop(1, rows - 1, inner, 0)

        @pl.when(me > 0)
        def _():
            down(step).wait_recv()
            up(step).wait_send()

        @pl.when(me < slabs - 1)
        def _():
            up(step).wait_recv()
            down(step).wait_send()

        update(step, 0, lambda s: halo[step, 0, s], lambda s: buf[now, 1, s])
        update(step, rows - 1, lambda s: buf[now, rows - 2, s], lambda s: halo[step, 1, s])
        if step < STEPS - 1:
            send(step + 1)

    end = STEPS % 2

    def products(i, acc):
        pair = jnp.concatenate([buf[end, 2 * i], buf[end, 2 * i + 1]], axis=1)
        return acc + dot_t(pair, pair)

    part[...] = lax.fori_loop(0, rows // 2, products, jnp.zeros((snaps, snaps), jnp.float32))

    def scatter(k):
        peer = lax.rem(me + k, slabs)
        return pltpu.make_async_remote_copy(
            src_ref=part.at[pl.ds(peer * share, share)], dst_ref=pieces.at[k],
            send_sem=rs_send.at[k], recv_sem=rs_recv.at[k], device_id=(place, peer), device_id_type=MESH)

    def gather(k):
        peer = lax.rem(me + k, slabs)
        return pltpu.make_async_remote_copy(
            src_ref=total, dst_ref=gram_ref.at[pl.ds(me * share, share)],
            send_sem=ag_send.at[k], recv_sem=ag_recv.at[k], device_id=(place, peer), device_id_type=MESH)

    for k in range(1, slabs):
        scatter(k).start()
    for r in range(rows):
        field_ref[r] = buf[end, r]
    acc = part[pl.ds(pl.multiple_of(me * share, 8), share)]
    for k in range(1, slabs):
        scatter(k).wait_recv()
        acc = acc + pieces[k]
    total[...] = acc
    for k in range(1, slabs):
        gather(k).start()
    gram_ref[pl.ds(pl.multiple_of(me * share, 8), share)] = acc
    for k in range(1, slabs):
        scatter(k).wait_send()
    for k in range(1, slabs):
        gather(k).wait()


def flow(slabs, x, coef, source, table, idx, count):
    rows, cols = coef.shape
    snaps = x.shape[0] // rows
    f32 = jnp.float32
    return pl.pallas_call(
        functools.partial(flow_kernel, slabs),
        out_shape=(jax.ShapeDtypeStruct((rows, snaps, cols), f32), jax.ShapeDtypeStruct((snaps, snaps), f32)),
        in_specs=[VMEM, VMEM, VMEM, VMEM, VMEM, SMEM],
        out_specs=(VMEM, VMEM),
        scratch_shapes=[
            pltpu.VMEM((2, rows, snaps, cols), f32),
            pltpu.VMEM((STEPS, 2, snaps, cols), f32),
            pltpu.VMEM((snaps, cols), f32),
            pltpu.VMEM((snaps, snaps), f32),
            pltpu.VMEM((slabs, snaps // slabs, snaps), f32),
            pltpu.VMEM((snaps // slabs, snaps), f32),
            pltpu.SemaphoreType.DMA((STEPS, 2)),
            pltpu.SemaphoreType.DMA((STEPS, 2)),
            pltpu.SemaphoreType.DMA((slabs,)),
            pltpu.SemaphoreType.DMA((slabs,)),
            pltpu.SemaphoreType.DMA((slabs,)),
            pltpu.SemaphoreType.DMA((slabs,)),
        ],
        compiler_params=pltpu.CompilerParams(collective_id=0, has_side_effects=True, vmem_limit_bytes=VMEM_LIMIT),
    )(x, coef, source, table, idx, count)


def eliminate(problems, outs):
    size = problems[0][0].shape[0]
    blocks = size // 8
    wide = 128
    sub = lax.broadcasted_iota(jnp.int32, (8, wide), 0)
    lane = lax.broadcasted_iota(jnp.int32, (8, wide), 1)

    def split(value):
        return tuple(value[8 * b : 8 * b + 8] for b in range(blocks))

    def padded(m):
        return jnp.concatenate([m, jnp.zeros((size, wide - size), jnp.float32)], axis=1)

    start = tuple((split(padded(m)), split(r)) for m, r in problems)

    def body(t, carry):
        states = [[list(ms), list(rs)] for ms, rs in carry]
        for k in range(8):
            for ms, rs in states:
                inv = 1.0 / ms[0][k : k + 1, k : k + 1]
                row_m = ms[0][k : k + 1] * inv
                row_r = rs[0][k : k + 1] * inv
                cols = [jnp.broadcast_to(ms[b][:, k : k + 1], (8, wide)) for b in range(blocks)]
                cols[0] = jnp.where(sub > k, cols[0], 0.0)
                for b in range(blocks):
                    ms[b] = ms[b] - cols[b] * row_m
                    rs[b] = rs[b] - cols[b] * row_r
        following = []
        for (ms, rs), out in zip(states, outs):
            pivots = jnp.sum(jnp.where(sub == lane, ms[0], 0.0), axis=1, keepdims=True)
            out[pl.ds(pl.multiple_of(8 * t, 8), 8), :] = rs[0] * lax.rsqrt(pivots)
            zero = jnp.zeros((8, wide), jnp.float32)
            moved = [pltpu.roll(m, wide - 8, 1) for m in ms[1:]] + [zero]
            following.append((tuple(moved), tuple(rs[1:] + [zero])))
        return tuple(following)

    lax.fori_loop(0, blocks, body, start)


def shifted(m):
    size = m.shape[0]
    eye = lax.broadcasted_iota(jnp.int32, m.shape, 0) == lax.broadcasted_iota(jnp.int32, m.shape, 1)
    trace = jnp.sum(jnp.where(eye, m, 0.0), keepdims=True)
    return m + jnp.where(eye, (0.0001 / size) * trace, 0.0)


def mixings(grams, omega_t, outs):
    size = omega_t.shape[0]
    moments = [shifted(dot_t(dot(omega_t, g), omega_t)) for g in grams]
    eliminate([(m, omega_t) for m in moments], outs)
    lefts = [out[...] for out in outs[: len(grams)]]
    inners = []
    for left, g in zip(lefts, grams):
        hmat = dot(left, g)
        inners.append(shifted(dot_t(hmat, hmat)))
    pad = jnp.zeros((size, 128 - size), jnp.float32)
    eliminate([(c, jnp.concatenate([c, pad], axis=1)) for c in inners], outs)
    return [dot(out[:, :size], left) for out, left in zip(outs, lefts)]


def leaf_kernel(places, field_ref, gram_ref, omega_ref, packed_ref, out0):
    rows, snaps, cols = field_ref.shape
    modes = omega_ref.shape[0]
    mixing = mixings([gram_ref[...]], omega_ref[...], [out0])[0]
    width = cols // places
    per = cols // width
    lane = lax.broadcasted_iota(jnp.int32, (modes, cols), 1) // width
    for group in range(rows // per):
        pieces = [dot(mixing, field_ref[group * per + j]) for j in range(per)]
        for q in range(places):
            total = jnp.zeros((modes, cols), jnp.float32)
            for j in range(per):
                turn = (j - q) % per * width
                moved = pltpu.roll(pieces[j], turn, 1) if turn else pieces[j]
                total = jnp.where(lane == j, moved, total)
            packed_ref[q, group] = total


def leaf(places, field, gram, omega_t):
    rows, _, cols = field.shape
    modes = omega_t.shape[0]
    return pl.pallas_call(
        functools.partial(leaf_kernel, places),
        out_shape=jax.ShapeDtypeStruct((places, rows // places, modes, cols), jnp.float32),
        in_specs=[VMEM] * 3,
        out_specs=VMEM,
        scratch_shapes=[pltpu.VMEM((modes, 128), jnp.float32)],
        compiler_params=pltpu.CompilerParams(vmem_limit_bytes=VMEM_LIMIT),
    )(field, gram, omega_t)


def cross_kernel(slabs, places, packed_ref, all_ref, gram_ref, part, pieces, total, extra, *sems):
    a_send, a_recv, rs_send, rs_recv, px_send, px_recv, ag_send, ag_recv = sems
    _, groups, modes, cols = packed_ref.shape
    me = lax.axis_index("slab")
    place = lax.axis_index("param")
    count = places // 2
    share = part.shape[0] // slabs
    size = 2 * modes

    barrier = pltpu.get_barrier_semaphore()
    for k in range(1, slabs):
        pl.semaphore_signal(barrier, inc=1, device_id=(place, lax.rem(me + k, slabs)), device_id_type=MESH)
    for k in range(1, places):
        pl.semaphore_signal(barrier, inc=1, device_id=(lax.rem(place + k, places), me), device_id_type=MESH)
    pl.semaphore_wait(barrier, slabs + places - 2)

    def swap(k):
        peer = lax.rem(place + k, places)
        return pltpu.make_async_remote_copy(
            src_ref=packed_ref.at[peer], dst_ref=all_ref.at[place],
            send_sem=a_send.at[k], recv_sem=a_recv.at[k], device_id=(peer, me), device_id_type=MESH)

    for k in range(1, places):
        swap(k).start()
    for group in range(groups):
        all_ref[place, group] = packed_ref[place, group]
    for k in range(1, places):
        swap(k).wait()

    def stacked(i):
        return jnp.concatenate(
            [jnp.concatenate([all_ref[2 * i + h, g] for g in range(groups)], axis=1) for h in range(2)], axis=0)

    at = 0
    for i in range(count):
        for j in range(i, count):
            part[at * size : (at + 1) * size] = dot_t(stacked(i), stacked(j))
            at += 1

    def scatter(k):
        peer = lax.rem(me + k, slabs)
        return pltpu.make_async_remote_copy(
            src_ref=part.at[pl.ds(peer * share, share)], dst_ref=pieces.at[k],
            send_sem=rs_send.at[k], recv_sem=rs_recv.at[k], device_id=(place, peer), device_id_type=MESH)

    def across(k):
        return pltpu.make_async_remote_copy(
            src_ref=extra.at[place], dst_ref=extra.at[place],
            send_sem=px_send.at[k], recv_sem=px_recv.at[k],
            device_id=(lax.rem(place + k, places), me), device_id_type=MESH)

    def gather(k):
        peer = lax.rem(me + k, slabs)
        return pltpu.make_async_remote_copy(
            src_ref=total, dst_ref=gram_ref.at[pl.ds(me * share, share)],
            send_sem=ag_send.at[k], recv_sem=ag_recv.at[k], device_id=(place, peer), device_id_type=MESH)

    for k in range(1, slabs):
        scatter(k).start()
    acc = part[pl.ds(pl.multiple_of(me * share, 8), share)]
    for k in range(1, slabs):
        scatter(k).wait_recv()
        acc = acc + pieces[k]
    extra[place] = acc
    for k in range(1, places):
        across(k).start()
    for k in range(1, places):
        across(k).wait()
    acc = extra[0]
    for k in range(1, places):
        acc = acc + extra[k]
    total[...] = acc
    for k in range(1, slabs):
        gather(k).start()
    gram_ref[pl.ds(pl.multiple_of(me * share, 8), share)] = acc
    for k in range(1, slabs):
        scatter(k).wait_send()
    for k in range(1, slabs):
        gather(k).wait()


def cross(slabs, places, packed):
    _, groups, modes, cols = packed.shape
    count = places // 2
    tall = count * (count + 1) // 2 * 2 * modes
    share = tall // slabs
    f32 = jnp.float32
    wide = 2 * modes
    return pl.pallas_call(
        functools.partial(cross_kernel, slabs, places),
        out_shape=(jax.ShapeDtypeStruct(packed.shape, f32), jax.ShapeDtypeStruct((tall, wide), f32)),
        in_specs=[VMEM],
        out_specs=(VMEM, VMEM),
        scratch_shapes=[
            pltpu.VMEM((tall, wide), f32),
            pltpu.VMEM((slabs, share, wide), f32),
            pltpu.VMEM((share, wide), f32),
            pltpu.VMEM((places, share, wide), f32),
        ] + [pltpu.SemaphoreType.DMA((n,)) for n in (places, places, slabs, slabs, places, places, slabs, slabs)],
        compiler_params=pltpu.CompilerParams(collective_id=1, has_side_effects=True, vmem_limit_bytes=VMEM_LIMIT),
    )(packed)


def merge_kernel(all_ref, gram_ref, omega_ref, modes_ref, *outs):
    places, groups, modes, cols = all_ref.shape
    size = 2 * modes
    count = places // 2
    blocks = {}
    for i in range(count):
        for j in range(i, count):
            at = len(blocks) * size
            blocks[i, j] = gram_ref[at : at + size]
    trees = None
    level = 0
    while count:
        mixes = []
        for at in range(0, count, 2):
            some = range(at, min(at + 2, count))
            mixes += mixings([0.5 * blocks[i, i] for i in some], omega_ref[level], outs)
        mixes = [0.5**0.5 * m for m in mixes]
        if trees is None:
            trees = mixes
        else:
            trees = [
                jnp.concatenate([dot(m[:, :modes], trees[2 * i]), dot(m[:, modes:], trees[2 * i + 1])], axis=1)
                for i, m in enumerate(mixes)
            ]
        count //= 2
        level += 1
        if count:
            fine = {}
            for i in range(2 * count):
                for j in range(i, 2 * count):
                    fine[i, j] = dot_t(dot(mixes[i], blocks[i, j]), mixes[j])
            blocks = {}
            for i in range(count):
                for j in range(i, count):
                    lower = fine[2 * i + 1, 2 * j] if i < j else jnp.transpose(fine[2 * i, 2 * j + 1])
                    top = jnp.concatenate([fine[2 * i, 2 * j], fine[2 * i, 2 * j + 1]], axis=1)
                    bottom = jnp.concatenate([lower, fine[2 * i + 1, 2 * j + 1]], axis=1)
                    blocks[i, j] = jnp.concatenate([top, bottom], axis=0)
    tree = trees[0]
    for group in range(groups):
        stacked = jnp.concatenate([all_ref[i, group] for i in range(places)], axis=0)
        modes_ref[group] = dot(tree, stacked)


def merge(every, gram, omega_t):
    _, groups, modes, cols = every.shape
    return pl.pallas_call(
        merge_kernel,
        out_shape=jax.ShapeDtypeStruct((groups, modes, cols), jnp.float32),
        in_specs=[VMEM] * 3,
        out_specs=VMEM,
        scratch_shapes=[pltpu.VMEM((modes, 128), jnp.float32)] * 2,
        compiler_params=pltpu.CompilerParams(vmem_limit_bytes=VMEM_LIMIT),
    )(every, gram, omega_t)


def per_device(slabs, places, init_state, coef, source, amplitudes, sample_idx, step_counts, sketch_signs):
    _, snaps, rows, cols = init_state.shape
    signs = sketch_signs.astype(jnp.float32)
    omega_t = (2.0 * jnp.swapaxes(signs, 1, 2) - 1.0) / math.sqrt(sketch_signs.shape[1])
    field, gram = flow(slabs, init_state.reshape(snaps * rows, cols), coef[0], source,
                       amplitudes.reshape(1, -1), sample_idx, step_counts)
    packed = leaf(places, field, gram, omega_t[0])
    every, grams = cross(slabs, places, packed)
    out = merge(every, grams, omega_t[1:])
    modes = out.shape[1]
    return jnp.swapaxes(out, 0, 1).reshape(modes, rows, cols // places)


def solution(mesh):
    return jax.shard_map(
        functools.partial(per_device, mesh.shape["slab"], mesh.shape["param"]),
        mesh=mesh,
        in_specs=(
            P("param", None, "slab", None),
            P("param", "slab", None),
            P("slab", None),
            P(),
            P("param", None),
            P("param"),
            P(),
        ),
        out_specs=P(None, "slab", "param"),
        check_vma=False,
    )
```

```python
import functools
import math

import jax
import jax.numpy as jnp
from jax import lax
from jax.experimental import pallas as pl
from jax.experimental.pallas import tpu as pltpu
from jax.sharding import PartitionSpec as P

STEPS = 8
HALO = 2
MESH = pl.DeviceIdType.MESH
HIGHEST = lax.Precision.HIGHEST
VMEM_LIMIT = 48 * 1024 * 1024
VMEM = pl.BlockSpec(memory_space=pltpu.VMEM)
SMEM = pl.BlockSpec(memory_space=pltpu.SMEM)


def dot(a, b):
    return lax.dot_general(a, b, (((1,), (0,)), ((), ())), precision=HIGHEST, preferred_element_type=jnp.float32)


def dot_t(a, b):
    return lax.dot_general(a, b, (((1,), (1,)), ((), ())), precision=HIGHEST, preferred_element_type=jnp.float32)


def flow_kernel(slabs, x_ref, coef_ref, source_ref, table_ref, idx_ref, count_ref, field_ref, gram_ref,
                buf, halo, local, nearby, amp_ref, part, pieces, total, near_send, near_recv, halo_send, halo_recv, rs_send, rs_recv, ag_send, ag_recv):
    rows, cols = coef_ref.shape
    snaps = gram_ref.shape[0]
    share = snaps // slabs
    me = lax.axis_index("slab")
    place = lax.axis_index("param")
    peers = [lax.rem(me + k, slabs) for k in range(1, slabs)]

    barrier = pltpu.get_barrier_semaphore()
    for peer in peers:
        pl.semaphore_signal(barrier, inc=1, device_id=(place, peer), device_id_type=MESH)

    for r in range(rows):
        buf[0, HALO + r] = x_ref[pl.ds(r, snaps, stride=rows), :]

    table = jnp.broadcast_to(table_ref[...], (8, table_ref.shape[1]))
    entry = lax.broadcasted_iota(jnp.int32, (table_ref.shape[1], snaps), 0)
    picks = jnp.where(entry == idx_ref[...], 1.0, 0.0)
    amp_row = 0.1 * dot(table, picks)[0:1]
    amp_ref[...] = jnp.transpose(jnp.broadcast_to(amp_row, (cols, snaps)))

    nothing = jnp.zeros((HALO, snaps, cols), jnp.float32)
    local[0] = coef_ref[...]
    local[1] = source_ref[...]

    @pl.when(me == 0)
    def _():
        nearby[0] = jnp.zeros((2, rows, cols), jnp.float32)
        for turn in range(STEPS // HALO):
            halo[turn, 0] = nothing

    @pl.when(me == slabs - 1)
    def _():
        nearby[1] = jnp.zeros((2, rows, cols), jnp.float32)
        for turn in range(STEPS // HALO):
            halo[turn, 1] = nothing

    pl.semaphore_wait(barrier, slabs - 1)
    after, before = lax.rem(me + 1, slabs), lax.rem(me + slabs - 1, slabs)

    def hand(src, dst, sems, target):
        return pltpu.make_async_remote_copy(
            src_ref=src, dst_ref=dst, send_sem=sems[0], recv_sem=sems[1],
            device_id=(place, target), device_id_type=MESH)

    def down(turn):
        return hand(buf.at[turn * HALO % 2, pl.ds(rows, HALO)], halo.at[turn, 0],
                    (halo_send.at[turn, 0], halo_recv.at[turn, 0]), after)

    def up(turn):
        return hand(buf.at[turn * HALO % 2, pl.ds(HALO, HALO)], halo.at[turn, 1],
                    (halo_send.at[turn, 1], halo_recv.at[turn, 1]), before)

    def down_rates():
        return hand(local, nearby.at[0], (near_send.at[0], near_recv.at[0]), after)

    def up_rates():
        return hand(local, nearby.at[1], (near_send.at[1], near_recv.at[1]), before)

    def send(turn):
        @pl.when(me < slabs - 1)
        def _():
            down(turn).start()
            if turn == 0:
                down_rates().start()

        @pl.when(me > 0)
        def _():
            up(turn).start()
            if turn == 0:
                up_rates().start()

    def settle(turn):
        @pl.when(me > 0)
        def _():
            down(turn).wait_recv()
            up(turn).wait_send()
            if turn == 0:
                down_rates().wait_recv()
                up_rates().wait_send()

        @pl.when(me < slabs - 1)
        def _():
            up(turn).wait_recv()
            down(turn).wait_send()
            if turn == 0:
                up_rates().wait_recv()
                down_rates().wait_send()

    count = count_ref[0]
    chunk = 32
    lane = lax.broadcasted_iota(jnp.int32, (chunk, cols), 1)
    first, last = lane == 0, lane == cols - 1

    def update(step, r, read, rates):
        later = (step + 1) % 2
        active = jnp.where(step < count, 1.0, 0.0)
        rate = rates[0] * active
        force = rates[1] * active
        for c in range(0, snaps, chunk):
            s = pl.ds(c, chunk)
            f = read(r, s)
            left = jnp.where(first, 0.0, pltpu.roll(f, 1, 1))
            right = jnp.where(last, 0.0, pltpu.roll(f, cols - 1, 1))
            lap = read(r + 1, s) + read(r - 1, s) + right + left - 4.0 * f
            th = jnp.tanh(f)
            buf[later, HALO + r, s] = f + rate * (1.0 + 0.5 * (th * th)) * lap + amp_ref[s] * force

    def edge(step, r):
        turn, i = step // HALO, step % HALO

        def read(at, s):
            if i == 0 and at < 0:
                return halo[turn, 0, HALO + at, s]
            if i == 0 and at >= rows:
                return halo[turn, 1, at - rows, s]
            return buf[step % 2, HALO + at, s]

        if r < 0:
            rates = [nearby[0, n, rows + r : rows + r + 1] for n in range(2)]
        elif r >= rows:
            rates = [nearby[1, n, r - rows : r - rows + 1] for n in range(2)]
        else:
            rates = [local[n, r : r + 1] for n in range(2)]
        update(step, r, read, rates)

    send(0)
    for turn in range(STEPS // HALO):
        for i in range(HALO):
            step = turn * HALO + i

            def inner(r, carry):
                update(step, r, lambda at, s: buf[step % 2, HALO + at, s], [local[n, pl.ds(r, 1)] for n in range(2)])
                return carry

            lax.fori_loop(1 + i, rows - 1 - i, inner, 0)
        settle(turn)
        for i in range(HALO):
            step = turn * HALO + i
            for r in list(range(i + 1 - HALO, 1 + i)) + list(range(rows - 1 - i, rows + HALO - 1 - i)):
                edge(step, r)
        if turn < STEPS // HALO - 1:
            send(turn + 1)

    end = STEPS % 2

    def products(i, acc):
        pair = jnp.concatenate([buf[end, HALO + 2 * i], buf[end, HALO + 2 * i + 1]], axis=1)
        return acc + dot_t(pair, pair)

    part[...] = lax.fori_loop(0, rows // 2, products, jnp.zeros((snaps, snaps), jnp.float32))

    def scatter(k):
        peer = lax.rem(me + k, slabs)
        return pltpu.make_async_remote_copy(
            src_ref=part.at[pl.ds(peer * share, share)], dst_ref=pieces.at[k],
            send_sem=rs_send.at[k], recv_sem=rs_recv.at[k], device_id=(place, peer), device_id_type=MESH)

    def gather(k):
        peer = lax.rem(me + k, slabs)
        return pltpu.make_async_remote_copy(
            src_ref=total, dst_ref=gram_ref.at[pl.ds(me * share, share)],
            send_sem=ag_send.at[k], recv_sem=ag_recv.at[k], device_id=(place, peer), device_id_type=MESH)

    for k in range(1, slabs):
        scatter(k).start()
    for r in range(rows):
        field_ref[r] = buf[end, HALO + r]
    acc = part[pl.ds(pl.multiple_of(me * share, 8), share)]
    for k in range(1, slabs):
        scatter(k).wait_recv()
        acc = acc + pieces[k]
    total[...] = acc
    for k in range(1, slabs):
        gather(k).start()
    gram_ref[pl.ds(pl.multiple_of(me * share, 8), share)] = acc
    for k in range(1, slabs):
        scatter(k).wait_send()
    for k in range(1, slabs):
        gather(k).wait()


def flow(slabs, x, coef, source, table, idx, count):
    rows, cols = coef.shape
    snaps = x.shape[0] // rows
    f32 = jnp.float32
    return pl.pallas_call(
        functools.partial(flow_kernel, slabs),
        out_shape=(jax.ShapeDtypeStruct((rows, snaps, cols), f32), jax.ShapeDtypeStruct((snaps, snaps), f32)),
        in_specs=[VMEM, VMEM, VMEM, VMEM, VMEM, SMEM],
        out_specs=(VMEM, VMEM),
        scratch_shapes=[
            pltpu.VMEM((2, rows + 2 * HALO, snaps, cols), f32),
            pltpu.VMEM((STEPS // HALO, 2, HALO, snaps, cols), f32),
            pltpu.VMEM((2, rows, cols), f32),
            pltpu.VMEM((2, 2, rows, cols), f32),
            pltpu.VMEM((snaps, cols), f32),
            pltpu.VMEM((snaps, snaps), f32),
            pltpu.VMEM((slabs, snaps // slabs, snaps), f32),
            pltpu.VMEM((snaps // slabs, snaps), f32),
            pltpu.SemaphoreType.DMA((2,)),
            pltpu.SemaphoreType.DMA((2,)),
            pltpu.SemaphoreType.DMA((STEPS // HALO, 2)),
            pltpu.SemaphoreType.DMA((STEPS // HALO, 2)),
            pltpu.SemaphoreType.DMA((slabs,)),
            pltpu.SemaphoreType.DMA((slabs,)),
            pltpu.SemaphoreType.DMA((slabs,)),
            pltpu.SemaphoreType.DMA((slabs,)),
        ],
        compiler_params=pltpu.CompilerParams(collective_id=0, has_side_effects=True, vmem_limit_bytes=VMEM_LIMIT),
    )(x, coef, source, table, idx, count)


def eliminate(problems, outs):
    size = problems[0][0].shape[0]
    blocks = size // 8
    wide = 128
    sub = lax.broadcasted_iota(jnp.int32, (8, wide), 0)

    def split(value):
        return tuple(value[8 * b : 8 * b + 8] for b in range(blocks))

    def padded(m):
        return jnp.concatenate([m, jnp.zeros((size, wide - size), jnp.float32)], axis=1)

    start = tuple((split(padded(m)), split(r)) for m, r in problems)

    def spread(value, k):
        return jnp.broadcast_to(value[k : k + 1], (8, wide))

    def body(t, carry):
        states = []
        for ms, rs in carry:
            cols = [jnp.broadcast_to(ms[0][:, k : k + 1], (8, wide)) for k in range(8)]
            zero = jnp.zeros((8, wide), jnp.float32)
            states.append([ms[0], rs[0], cols, zero, zero])
        for k in range(8):
            for state in states:
                m0, r0, cols, done, scale = state
                pivot = spread(cols[k], k)
                inv = 1.0 / pivot
                factor = jnp.where(sub == k, 0.0, cols[k] * inv)
                done = jnp.where(sub == k, r0 * lax.rsqrt(pivot), done)
                scale = jnp.where(sub == k, inv, scale)
                cols = [c if j <= k else c - factor * spread(c, k) for j, c in enumerate(cols)]
                state[:] = [m0 - factor * spread(m0, k), r0 - factor * spread(r0, k), cols, done, scale]
        following = []
        for (ms, rs), (m0, r0, _, done, scale), out in zip(carry, states, outs):
            out[pl.ds(pl.multiple_of(8 * t, 8), 8), :] = done
            rows_m = [spread(m0 * scale, k) for k in range(8)]
            rows_r = [spread(r0 * scale, k) for k in range(8)]
            next_m, next_r = [], []
            for m, r in zip(ms[1:], rs[1:]):
                less_m = less_r = 0.0
                for k in range(8):
                    col = jnp.broadcast_to(m[:, k : k + 1], (8, wide))
                    less_m, less_r = less_m + col * rows_m[k], less_r + col * rows_r[k]
                next_m.append(pltpu.roll(m - less_m, wide - 8, 1))
                next_r.append(r - less_r)
            zero = jnp.zeros((8, wide), jnp.float32)
            following.append((tuple(next_m + [zero]), tuple(next_r + [zero])))
        return tuple(following)

    lax.fori_loop(0, blocks, body, start)


def shifted(m):
    size = m.shape[0]
    eye = lax.broadcasted_iota(jnp.int32, m.shape, 0) == lax.broadcasted_iota(jnp.int32, m.shape, 1)
    trace = jnp.sum(jnp.where(eye, m, 0.0), keepdims=True)
    return m + jnp.where(eye, (0.0001 / size) * trace, 0.0)


def mixings(grams, omega_t, outs):
    size = omega_t.shape[0]
    moments = [shifted(dot_t(dot(omega_t, g), omega_t)) for g in grams]
    eliminate([(m, omega_t) for m in moments], outs)
    lefts = [out[...] for out in outs[: len(grams)]]
    inners = []
    for left, g in zip(lefts, grams):
        hmat = dot(left, g)
        inners.append(shifted(dot_t(hmat, hmat)))
    pad = jnp.zeros((size, 128 - size), jnp.float32)
    eliminate([(c, jnp.concatenate([c, pad], axis=1)) for c in inners], outs)
    return [dot(out[:, :size], left) for out, left in zip(outs, lefts)]


def leaf_kernel(places, field_ref, gram_ref, omega_ref, packed_ref, out0):
    rows, snaps, cols = field_ref.shape
    modes = omega_ref.shape[0]
    mixing = mixings([gram_ref[...]], omega_ref[...], [out0])[0]
    width = cols // places
    per = cols // width
    lane = lax.broadcasted_iota(jnp.int32, (modes, cols), 1) // width
    for group in range(rows // per):
        pieces = [dot(mixing, field_ref[group * per + j]) for j in range(per)]
        for q in range(places):
            total = jnp.zeros((modes, cols), jnp.float32)
            for j in range(per):
                turn = (j - q) % per * width
                moved = pltpu.roll(pieces[j], turn, 1) if turn else pieces[j]
                total = jnp.where(lane == j, moved, total)
            packed_ref[q, group] = total


def leaf(places, field, gram, omega_t):
    rows, _, cols = field.shape
    modes = omega_t.shape[0]
    return pl.pallas_call(
        functools.partial(leaf_kernel, places),
        out_shape=jax.ShapeDtypeStruct((places, rows // places, modes, cols), jnp.float32),
        in_specs=[VMEM] * 3,
        out_specs=VMEM,
        scratch_shapes=[pltpu.VMEM((modes, 128), jnp.float32)],
        compiler_params=pltpu.CompilerParams(vmem_limit_bytes=VMEM_LIMIT),
    )(field, gram, omega_t)


def cross_kernel(slabs, places, packed_ref, all_ref, gram_ref, part, pieces, total, extra, *sems):
    a_send, a_recv, rs_send, rs_recv, px_send, px_recv, ag_send, ag_recv = sems
    _, groups, modes, cols = packed_ref.shape
    me = lax.axis_index("slab")
    place = lax.axis_index("param")
    count = places // 2
    share = part.shape[0] // slabs
    size = 2 * modes

    barrier = pltpu.get_barrier_semaphore()
    for k in range(1, slabs):
        pl.semaphore_signal(barrier, inc=1, device_id=(place, lax.rem(me + k, slabs)), device_id_type=MESH)
    for k in range(1, places):
        pl.semaphore_signal(barrier, inc=1, device_id=(lax.rem(place + k, places), me), device_id_type=MESH)
    pl.semaphore_wait(barrier, slabs + places - 2)

    def swap(k):
        peer = lax.rem(place + k, places)
        return pltpu.make_async_remote_copy(
            src_ref=packed_ref.at[peer], dst_ref=all_ref.at[place],
            send_sem=a_send.at[k], recv_sem=a_recv.at[k], device_id=(peer, me), device_id_type=MESH)

    for k in range(1, places):
        swap(k).start()
    for group in range(groups):
        all_ref[place, group] = packed_ref[place, group]
    for k in range(1, places):
        swap(k).wait()

    def stacked(i):
        return jnp.concatenate(
            [jnp.concatenate([all_ref[2 * i + h, g] for g in range(groups)], axis=1) for h in range(2)], axis=0)

    at = 0
    for i in range(count):
        for j in range(i, count):
            part[at * size : (at + 1) * size] = dot_t(stacked(i), stacked(j))
            at += 1

    def scatter(k):
        peer = lax.rem(me + k, slabs)
        return pltpu.make_async_remote_copy(
            src_ref=part.at[pl.ds(peer * share, share)], dst_ref=pieces.at[k],
            send_sem=rs_send.at[k], recv_sem=rs_recv.at[k], device_id=(place, peer), device_id_type=MESH)

    def across(k):
        return pltpu.make_async_remote_copy(
            src_ref=extra.at[place], dst_ref=extra.at[place],
            send_sem=px_send.at[k], recv_sem=px_recv.at[k],
            device_id=(lax.rem(place + k, places), me), device_id_type=MESH)

    def gather(k):
        peer = lax.rem(me + k, slabs)
        return pltpu.make_async_remote_copy(
            src_ref=total, dst_ref=gram_ref.at[pl.ds(me * share, share)],
            send_sem=ag_send.at[k], recv_sem=ag_recv.at[k], device_id=(place, peer), device_id_type=MESH)

    for k in range(1, slabs):
        scatter(k).start()
    acc = part[pl.ds(pl.multiple_of(me * share, 8), share)]
    for k in range(1, slabs):
        scatter(k).wait_recv()
        acc = acc + pieces[k]
    extra[place] = acc
    for k in range(1, places):
        across(k).start()
    for k in range(1, places):
        across(k).wait()
    acc = extra[0]
    for k in range(1, places):
        acc = acc + extra[k]
    total[...] = acc
    for k in range(1, slabs):
        gather(k).start()
    gram_ref[pl.ds(pl.multiple_of(me * share, 8), share)] = acc
    for k in range(1, slabs):
        scatter(k).wait_send()
    for k in range(1, slabs):
        gather(k).wait()


def cross(slabs, places, packed):
    _, groups, modes, cols = packed.shape
    count = places // 2
    tall = count * (count + 1) // 2 * 2 * modes
    share = tall // slabs
    f32 = jnp.float32
    wide = 2 * modes
    return pl.pallas_call(
        functools.partial(cross_kernel, slabs, places),
        out_shape=(jax.ShapeDtypeStruct(packed.shape, f32), jax.ShapeDtypeStruct((tall, wide), f32)),
        in_specs=[VMEM],
        out_specs=(VMEM, VMEM),
        scratch_shapes=[
            pltpu.VMEM((tall, wide), f32),
            pltpu.VMEM((slabs, share, wide), f32),
            pltpu.VMEM((share, wide), f32),
            pltpu.VMEM((places, share, wide), f32),
        ] + [pltpu.SemaphoreType.DMA((n,)) for n in (places, places, slabs, slabs, places, places, slabs, slabs)],
        compiler_params=pltpu.CompilerParams(collective_id=1, has_side_effects=True, vmem_limit_bytes=VMEM_LIMIT),
    )(packed)


def merge_kernel(all_ref, gram_ref, omega_ref, modes_ref, *outs):
    places, groups, modes, cols = all_ref.shape
    size = 2 * modes
    count = places // 2
    blocks = {}
    for i in range(count):
        for j in range(i, count):
            at = len(blocks) * size
            blocks[i, j] = gram_ref[at : at + size]
    trees = None
    level = 0
    while count:
        mixes = []
        for at in range(0, count, 2):
            some = range(at, min(at + 2, count))
            mixes += mixings([0.5 * blocks[i, i] for i in some], omega_ref[level], outs)
        mixes = [0.5**0.5 * m for m in mixes]
        if trees is None:
            trees = mixes
        else:
            trees = [
                jnp.concatenate([dot(m[:, :modes], trees[2 * i]), dot(m[:, modes:], trees[2 * i + 1])], axis=1)
                for i, m in enumerate(mixes)
            ]
        count //= 2
        level += 1
        if count:
            fine = {}
            for i in range(2 * count):
                for j in range(i, 2 * count):
                    fine[i, j] = dot_t(dot(mixes[i], blocks[i, j]), mixes[j])
            blocks = {}
            for i in range(count):
                for j in range(i, count):
                    lower = fine[2 * i + 1, 2 * j] if i < j else jnp.transpose(fine[2 * i, 2 * j + 1])
                    top = jnp.concatenate([fine[2 * i, 2 * j], fine[2 * i, 2 * j + 1]], axis=1)
                    bottom = jnp.concatenate([lower, fine[2 * i + 1, 2 * j + 1]], axis=1)
                    blocks[i, j] = jnp.concatenate([top, bottom], axis=0)
    tree = trees[0]
    for group in range(groups):
        stacked = jnp.concatenate([all_ref[i, group] for i in range(places)], axis=0)
        modes_ref[group] = dot(tree, stacked)


def merge(every, gram, omega_t):
    _, groups, modes, cols = every.shape
    return pl.pallas_call(
        merge_kernel,
        out_shape=jax.ShapeDtypeStruct((groups, modes, cols), jnp.float32),
        in_specs=[VMEM] * 3,
        out_specs=VMEM,
        scratch_shapes=[pltpu.VMEM((modes, 128), jnp.float32)] * 2,
        compiler_params=pltpu.CompilerParams(vmem_limit_bytes=VMEM_LIMIT),
    )(every, gram, omega_t)


def per_device(slabs, places, init_state, coef, source, amplitudes, sample_idx, step_counts, sketch_signs):
    _, snaps, rows, cols = init_state.shape
    signs = sketch_signs.astype(jnp.float32)
    omega_t = (2.0 * jnp.swapaxes(signs, 1, 2) - 1.0) / math.sqrt(sketch_signs.shape[1])
    field, gram = flow(slabs, init_state.reshape(snaps * rows, cols), coef[0], source,
                       amplitudes.reshape(1, -1), sample_idx, step_counts)
    packed = leaf(places, field, gram, omega_t[0])
    every, grams = cross(slabs, places, packed)
    out = merge(every, grams, omega_t[1:])
    modes = out.shape[1]
    return jnp.swapaxes(out, 0, 1).reshape(modes, rows, cols // places)


def solution(mesh):
    return jax.shard_map(
        functools.partial(per_device, mesh.shape["slab"], mesh.shape["param"]),
        mesh=mesh,
        in_specs=(
            P("param", None, "slab", None),
            P("param", "slab", None),
            P("slab", None),
            P(),
            P("param", None),
            P("param"),
            P(),
        ),
        out_specs=P(None, "slab", "param"),
        check_vma=False,
    )
```

```python
import functools
import math

import jax
import jax.numpy as jnp
from jax import lax
from jax.experimental import pallas as pl
from jax.experimental.pallas import tpu as pltpu
from jax.sharding import PartitionSpec as P

STEPS = 8
HALO = 2
FUSED = False
MESH = pl.DeviceIdType.MESH
HIGHEST = lax.Precision.HIGHEST
VMEM_LIMIT = 48 * 1024 * 1024
VMEM = pl.BlockSpec(memory_space=pltpu.VMEM)
SMEM = pl.BlockSpec(memory_space=pltpu.SMEM)


def dot(a, b):
    return lax.dot_general(a, b, (((1,), (0,)), ((), ())), precision=HIGHEST, preferred_element_type=jnp.float32)


def dot_t(a, b):
    return lax.dot_general(a, b, (((1,), (1,)), ((), ())), precision=HIGHEST, preferred_element_type=jnp.float32)


def flow_kernel(slabs, places, x_ref, coef_ref, source_ref, table_ref, idx_ref, count_ref, omega_ref, *refs):
    if FUSED:
        modes_ref, every_ref, own_ref, cross_ref, *refs = refs
    else:
        every_ref, own_ref, cross_ref, *refs = refs
    (buf, halo, local, nearby, amp_ref, part, pieces, total, packed, fields, grams, mixes, tall, bits, mine, extra,
     out0, out1, near_send, near_recv, halo_send, halo_recv, rs_send, rs_recv, ag_send, ag_recv, x_send, x_recv,
     g_send, g_recv, m_send, m_recv, rt_send, rt_recv, px_send, px_recv, at_send, at_recv) = refs
    rows, cols = coef_ref.shape
    snaps = part.shape[0]
    modes = omega_ref.shape[1]
    groups = rows // places
    count_pairs = places // 2
    share = snaps // slabs
    me = lax.axis_index("slab")
    place = lax.axis_index("param")
    peers = [lax.rem(me + k, slabs) for k in range(1, slabs)]

    barrier = pltpu.get_barrier_semaphore()
    for peer in peers:
        pl.semaphore_signal(barrier, inc=1, device_id=(place, peer), device_id_type=MESH)
    for k in range(1, places):
        pl.semaphore_signal(barrier, inc=1, device_id=(lax.rem(place + k, places), me), device_id_type=MESH)

    for r in range(rows):
        buf[0, HALO + r] = x_ref[pl.ds(r, snaps, stride=rows), :]

    table = jnp.broadcast_to(table_ref[...], (8, table_ref.shape[1]))
    entry = lax.broadcasted_iota(jnp.int32, (table_ref.shape[1], snaps), 0)
    picks = jnp.where(entry == idx_ref[...], 1.0, 0.0)
    amp_row = 0.1 * dot(table, picks)[0:1]
    amp_ref[...] = jnp.transpose(jnp.broadcast_to(amp_row, (cols, snaps)))

    nothing = jnp.zeros((HALO, snaps, cols), jnp.float32)
    local[0] = coef_ref[...]
    local[1] = source_ref[...]

    @pl.when(me == 0)
    def _():
        nearby[0] = jnp.zeros((2, rows, cols), jnp.float32)
        for turn in range(STEPS // HALO):
            halo[turn, 0] = nothing

    @pl.when(me == slabs - 1)
    def _():
        nearby[1] = jnp.zeros((2, rows, cols), jnp.float32)
        for turn in range(STEPS // HALO):
            halo[turn, 1] = nothing

    pl.semaphore_wait(barrier, slabs + places - 2)
    after, before = lax.rem(me + 1, slabs), lax.rem(me + slabs - 1, slabs)

    def hand(src, dst, sems, target):
        return pltpu.make_async_remote_copy(
            src_ref=src, dst_ref=dst, send_sem=sems[0], recv_sem=sems[1],
            device_id=(place, target), device_id_type=MESH)

    def down(turn):
        return hand(buf.at[turn * HALO % 2, pl.ds(rows, HALO)], halo.at[turn, 0],
                    (halo_send.at[turn, 0], halo_recv.at[turn, 0]), after)

    def up(turn):
        return hand(buf.at[turn * HALO % 2, pl.ds(HALO, HALO)], halo.at[turn, 1],
                    (halo_send.at[turn, 1], halo_recv.at[turn, 1]), before)

    def down_rates():
        return hand(local, nearby.at[0], (near_send.at[0], near_recv.at[0]), after)

    def up_rates():
        return hand(local, nearby.at[1], (near_send.at[1], near_recv.at[1]), before)

    def send(turn):
        @pl.when(me < slabs - 1)
        def _():
            down(turn).start()
            if turn == 0:
                down_rates().start()

        @pl.when(me > 0)
        def _():
            up(turn).start()
            if turn == 0:
                up_rates().start()

    def settle(turn):
        @pl.when(me > 0)
        def _():
            down(turn).wait_recv()
            up(turn).wait_send()
            if turn == 0:
                down_rates().wait_recv()
                up_rates().wait_send()

        @pl.when(me < slabs - 1)
        def _():
            up(turn).wait_recv()
            down(turn).wait_send()
            if turn == 0:
                up_rates().wait_recv()
                down_rates().wait_send()

    count = count_ref[0]
    chunk = 32
    lane = lax.broadcasted_iota(jnp.int32, (chunk, cols), 1)
    first, last = lane == 0, lane == cols - 1

    def update(step, r, read, rates):
        later = (step + 1) % 2
        active = jnp.where(step < count, 1.0, 0.0)
        rate = rates[0] * active
        force = rates[1] * active
        for c in range(0, snaps, chunk):
            s = pl.ds(c, chunk)
            f = read(r, s)
            left = jnp.where(first, 0.0, pltpu.roll(f, 1, 1))
            right = jnp.where(last, 0.0, pltpu.roll(f, cols - 1, 1))
            lap = read(r + 1, s) + read(r - 1, s) + right + left - 4.0 * f
            th = jnp.tanh(f)
            buf[later, HALO + r, s] = f + rate * (1.0 + 0.5 * (th * th)) * lap + amp_ref[s] * force

    def edge(step, r):
        turn, i = step // HALO, step % HALO

        def read(at, s):
            if i == 0 and at < 0:
                return halo[turn, 0, HALO + at, s]
            if i == 0 and at >= rows:
                return halo[turn, 1, at - rows, s]
            return buf[step % 2, HALO + at, s]

        if r < 0:
            rates = [nearby[0, n, rows + r : rows + r + 1] for n in range(2)]
        elif r >= rows:
            rates = [nearby[1, n, r - rows : r - rows + 1] for n in range(2)]
        else:
            rates = [local[n, r : r + 1] for n in range(2)]
        update(step, r, read, rates)

    send(0)
    for turn in range(STEPS // HALO):
        for i in range(HALO):
            step = turn * HALO + i

            def inner(r, carry):
                update(step, r, lambda at, s: buf[step % 2, HALO + at, s], [local[n, pl.ds(r, 1)] for n in range(2)])
                return carry

            lax.fori_loop(1 + i, rows - 1 - i, inner, 0)
        settle(turn)
        for i in range(HALO):
            step = turn * HALO + i
            for r in list(range(i + 1 - HALO, 1 + i)) + list(range(rows - 1 - i, rows + HALO - 1 - i)):
                edge(step, r)
        if turn < STEPS // HALO - 1:
            send(turn + 1)

    end = STEPS % 2

    width = cols // places
    slot = lax.broadcasted_iota(jnp.int32, (chunk, cols), 1) // width

    def pack(i, carry):
        group = i // (snaps // chunk)
        s = pl.ds(pl.multiple_of(i % (snaps // chunk) * chunk, chunk), chunk)
        parts = [buf[end, HALO + group * places + j, s] for j in range(places)]
        for q in range(places):
            whole = parts[q]
            for j in range(places):
                if j != q:
                    whole = jnp.where(slot == j, pltpu.roll(parts[j], (j - q) % places * width, 1), whole)
            packed[q, group, s] = whole
        return carry

    lax.fori_loop(0, groups * (snaps // chunk), pack, 0)

    def beside(k, src, dst, sems):
        return pltpu.make_async_remote_copy(
            src_ref=src, dst_ref=dst, send_sem=sems[0].at[k], recv_sem=sems[1].at[k],
            device_id=(lax.rem(place + k, places), me), device_id_type=MESH)

    def along(k, src, dst, sems):
        return pltpu.make_async_remote_copy(
            src_ref=src, dst_ref=dst, send_sem=sems[0].at[k], recv_sem=sems[1].at[k],
            device_id=(place, lax.rem(me + k, slabs)), device_id_type=MESH)

    def swap(k):
        return beside(k, packed.at[lax.rem(place + k, places)], fields.at[place], (x_send, x_recv))

    for k in range(1, places):
        swap(k).start()

    def products(i, acc):
        pair = jnp.concatenate([buf[end, HALO + 2 * i], buf[end, HALO + 2 * i + 1]], axis=1)
        return acc + dot_t(pair, pair)

    part[...] = lax.fori_loop(0, rows // 2, products, jnp.zeros((snaps, snaps), jnp.float32))

    def scatter(k):
        peer = lax.rem(me + k, slabs)
        return along(k, part.at[pl.ds(peer * share, share)], pieces.at[k], (rs_send, rs_recv))

    def gather(k):
        return along(k, total, grams.at[place, pl.ds(me * share, share)], (ag_send, ag_recv))

    for k in range(1, slabs):
        scatter(k).start()
    for group in range(groups):
        fields[place, group] = packed[place, group]
    acc = part[pl.ds(pl.multiple_of(me * share, 8), share)]
    for k in range(1, slabs):
        scatter(k).wait_recv()
        acc = acc + pieces[k]
    total[...] = acc
    for k in range(1, slabs):
        gather(k).start()
    grams[place, pl.ds(pl.multiple_of(me * share, 8), share)] = acc
    for k in range(1, slabs):
        gather(k).wait_recv()

    def lend(k):
        return beside(k, grams.at[place], grams.at[place], (g_send, g_recv))

    def share_mix(k):
        return beside(k, mixes.at[place], mixes.at[place], (m_send, m_recv))

    for k in range(1, places):
        lend(k).start()
    mixes[place] = mixings([grams[place]], omega_ref[0], [out0])[0]
    for k in range(1, places):
        share_mix(k).start()
    for k in range(1, places):
        swap(k).wait_recv()
    for k in range(1, places):
        share_mix(k).wait_recv()
    for i in range(places):
        for group in range(groups):
            every_ref[i, group] = dot(mixes[i], fields[i, group])

    def piece(i):
        return jnp.concatenate([every_ref[i, g] for g in range(groups)], axis=1)

    def stacked(i):
        return jnp.concatenate([piece(2 * i), piece(2 * i + 1)], axis=0)

    at = 0
    for i in range(count_pairs):
        for j in range(i + 1, count_pairs):
            tall[at : at + 2 * modes] = dot_t(stacked(i), stacked(j))
            at += 2 * modes
    for i in range(0, count_pairs, 2):
        tall[at : at + modes] = jnp.concatenate(
            [dot_t(piece(2 * h), piece(2 * h + 1)) for h in (i, i + 1)], axis=1)
        at += modes
    span = at // slabs

    def scatter_tall(k):
        peer = lax.rem(me + k, slabs)
        return along(k, tall.at[pl.ds(peer * span, span)], bits.at[k], (rt_send, rt_recv))

    def across(k):
        return beside(k, extra.at[place], extra.at[place], (px_send, px_recv))

    def gather_tall(k):
        return along(k, mine, cross_ref.at[pl.ds(me * span, span)], (at_send, at_recv))

    for k in range(1, slabs):
        scatter_tall(k).start()
    for k in range(1, places):
        lend(k).wait_recv()
    for i in range(places):
        own_ref[i] = dot_t(dot(mixes[i], grams[i]), mixes[i])
    acc = tall[pl.ds(pl.multiple_of(me * span, 8), span)]
    for k in range(1, slabs):
        scatter_tall(k).wait_recv()
        acc = acc + bits[k]
    extra[place] = acc
    for k in range(1, places):
        across(k).start()
    for k in range(1, places):
        across(k).wait_recv()
    acc = extra[0]
    for k in range(1, places):
        acc = acc + extra[k]
    mine[...] = acc
    for k in range(1, slabs):
        gather_tall(k).start()
    cross_ref[pl.ds(pl.multiple_of(me * span, 8), span)] = acc
    for k in range(1, slabs):
        scatter(k).wait_send()
        gather(k).wait_send()
        scatter_tall(k).wait_send()
    for k in range(1, places):
        swap(k).wait_send()
        lend(k).wait_send()
        share_mix(k).wait_send()
        across(k).wait_send()
    for k in range(1, slabs):
        gather_tall(k).wait()
    if FUSED:
        merge_levels(every_ref, own_ref, cross_ref, omega_ref, modes_ref, out0, out1)


def flow(slabs, places, x, coef, source, table, idx, count, omega_t):
    rows, cols = coef.shape
    snaps = x.shape[0] // rows
    modes = omega_t.shape[1]
    groups = rows // places
    pairs = places // 2
    high = pairs * (pairs - 1) // 2 * 2 * modes + pairs // 2 * modes
    f32 = jnp.float32

    def sems(*shape):
        return [pltpu.SemaphoreType.DMA(shape)] * 2

    inner = [(places, groups, modes, cols), (places, modes, modes), (high, 2 * modes)]
    result = [(groups, modes, cols)] if FUSED else inner
    out = pl.pallas_call(
        functools.partial(flow_kernel, slabs, places),
        out_shape=[jax.ShapeDtypeStruct(shape, f32) for shape in result],
        in_specs=[VMEM, VMEM, VMEM, VMEM, VMEM, SMEM, VMEM],
        out_specs=[VMEM] * len(result),
        scratch_shapes=([pltpu.VMEM(shape, f32) for shape in inner] if FUSED else []) + [
            pltpu.VMEM((2, rows + 2 * HALO, snaps, cols), f32),
            pltpu.VMEM((STEPS // HALO, 2, HALO, snaps, cols), f32),
            pltpu.VMEM((2, rows, cols), f32),
            pltpu.VMEM((2, 2, rows, cols), f32),
            pltpu.VMEM((snaps, cols), f32),
            pltpu.VMEM((snaps, snaps), f32),
            pltpu.VMEM((slabs, snaps // slabs, snaps), f32),
            pltpu.VMEM((snaps // slabs, snaps), f32),
            pltpu.VMEM((places, groups, snaps, cols), f32),
            pltpu.VMEM((places, groups, snaps, cols), f32),
            pltpu.VMEM((places, snaps, snaps), f32),
            pltpu.VMEM((places, modes, snaps), f32),
            pltpu.VMEM((high, 2 * modes), f32),
            pltpu.VMEM((slabs, high // slabs, 2 * modes), f32),
            pltpu.VMEM((high // slabs, 2 * modes), f32),
            pltpu.VMEM((places, high // slabs, 2 * modes), f32),
            pltpu.VMEM((modes, 128), f32),
            pltpu.VMEM((modes, 128), f32),
        ] + sems(2) + sems(STEPS // HALO, 2) + 2 * sems(slabs) + 3 * sems(places)
        + sems(slabs) + sems(places) + sems(slabs),
        compiler_params=pltpu.CompilerParams(collective_id=0, has_side_effects=True, vmem_limit_bytes=VMEM_LIMIT),
    )(x, coef, source, table, idx, count, omega_t)
    return out


def eliminate(problems, outs):
    size = problems[0][0].shape[0]
    blocks = size // 8
    wide = 128
    sub = lax.broadcasted_iota(jnp.int32, (8, wide), 0)

    def split(value):
        return tuple(value[8 * b : 8 * b + 8] for b in range(blocks))

    def padded(m):
        return jnp.concatenate([m, jnp.zeros((size, wide - size), jnp.float32)], axis=1)

    start = tuple((split(padded(m)), split(r)) for m, r in problems)

    def spread(value, k):
        return jnp.broadcast_to(value[k : k + 1], (8, wide))

    def body(t, carry):
        states = []
        for ms, rs in carry:
            cols = [jnp.broadcast_to(ms[0][:, k : k + 1], (8, wide)) for k in range(8)]
            zero = jnp.zeros((8, wide), jnp.float32)
            states.append([ms[0], rs[0], cols, zero, zero])
        for k in range(8):
            for state in states:
                m0, r0, cols, done, scale = state
                pivot = spread(cols[k], k)
                inv = 1.0 / pivot
                factor = jnp.where(sub == k, 0.0, cols[k] * inv)
                done = jnp.where(sub == k, r0 * lax.rsqrt(pivot), done)
                scale = jnp.where(sub == k, inv, scale)
                cols = [c if j <= k else c - factor * spread(c, k) for j, c in enumerate(cols)]
                state[:] = [m0 - factor * spread(m0, k), r0 - factor * spread(r0, k), cols, done, scale]
        following = []
        for (ms, rs), (m0, r0, _, done, scale), out in zip(carry, states, outs):
            out[pl.ds(pl.multiple_of(8 * t, 8), 8), :] = done
            rows_m = [spread(m0 * scale, k) for k in range(8)]
            rows_r = [spread(r0 * scale, k) for k in range(8)]
            next_m, next_r = [], []
            for m, r in zip(ms[1:], rs[1:]):
                less_m = less_r = 0.0
                for k in range(8):
                    col = jnp.broadcast_to(m[:, k : k + 1], (8, wide))
                    less_m, less_r = less_m + col * rows_m[k], less_r + col * rows_r[k]
                next_m.append(pltpu.roll(m - less_m, wide - 8, 1))
                next_r.append(r - less_r)
            zero = jnp.zeros((8, wide), jnp.float32)
            following.append((tuple(next_m + [zero]), tuple(next_r + [zero])))
        return tuple(following)

    lax.fori_loop(0, blocks, body, start)


def shifted(m):
    size = m.shape[0]
    eye = lax.broadcasted_iota(jnp.int32, m.shape, 0) == lax.broadcasted_iota(jnp.int32, m.shape, 1)
    trace = jnp.sum(jnp.where(eye, m, 0.0), keepdims=True)
    return m + jnp.where(eye, (0.0001 / size) * trace, 0.0)


def mixings(grams, omega_t, outs):
    size = omega_t.shape[0]
    moments = [shifted(dot_t(dot(omega_t, g), omega_t)) for g in grams]
    eliminate([(m, omega_t) for m in moments], outs)
    lefts = [out[...] for out in outs[: len(grams)]]
    inners = []
    for left, g in zip(lefts, grams):
        hmat = dot(left, g)
        inners.append(shifted(dot_t(hmat, hmat)))
    pad = jnp.zeros((size, 128 - size), jnp.float32)
    eliminate([(c, jnp.concatenate([c, pad], axis=1)) for c in inners], outs)
    return [dot(out[:, :size], left) for out, left in zip(outs, lefts)]


def merge_levels(every_ref, own_ref, cross_ref, omega_ref, modes_ref, *outs):
    places, groups, modes, cols = every_ref.shape
    size = 2 * modes
    count = places // 2
    blocks = {}
    at = 0
    for i in range(count):
        for j in range(i + 1, count):
            blocks[i, j] = cross_ref[at : at + size]
            at += size
    for i in range(0, count, 2):
        both = cross_ref[at : at + modes]
        at += modes
        for h in range(2):
            inner = both[:, h * modes : (h + 1) * modes]
            top = jnp.concatenate([own_ref[2 * (i + h)], inner], axis=1)
            bottom = jnp.concatenate([jnp.transpose(inner), own_ref[2 * (i + h) + 1]], axis=1)
            blocks[i + h, i + h] = jnp.concatenate([top, bottom], axis=0)
    trees = None
    level = 0
    while count:
        mixes = []
        for at in range(0, count, 2):
            some = range(at, min(at + 2, count))
            mixes += mixings([0.5 * blocks[i, i] for i in some], omega_ref[level + 1], outs)
        mixes = [0.5**0.5 * m for m in mixes]
        if trees is None:
            trees = mixes
        else:
            trees = [
                jnp.concatenate([dot(m[:, :modes], trees[2 * i]), dot(m[:, modes:], trees[2 * i + 1])], axis=1)
                for i, m in enumerate(mixes)
            ]
        count //= 2
        level += 1
        if count:
            fine = {}
            for i in range(2 * count):
                for j in range(i, 2 * count):
                    fine[i, j] = dot_t(dot(mixes[i], blocks[i, j]), mixes[j])
            blocks = {}
            for i in range(count):
                for j in range(i, count):
                    lower = fine[2 * i + 1, 2 * j] if i < j else jnp.transpose(fine[2 * i, 2 * j + 1])
                    top = jnp.concatenate([fine[2 * i, 2 * j], fine[2 * i, 2 * j + 1]], axis=1)
                    bottom = jnp.concatenate([lower, fine[2 * i + 1, 2 * j + 1]], axis=1)
                    blocks[i, j] = jnp.concatenate([top, bottom], axis=0)
    tree = trees[0]
    for group in range(groups):
        stacked = jnp.concatenate([every_ref[i, group] for i in range(places)], axis=0)
        modes_ref[group] = dot(tree, stacked)


def merge(every, own, cross, omega_t):
    _, groups, modes, cols = every.shape
    return pl.pallas_call(
        merge_levels,
        out_shape=jax.ShapeDtypeStruct((groups, modes, cols), jnp.float32),
        in_specs=[VMEM] * 4,
        out_specs=VMEM,
        scratch_shapes=[pltpu.VMEM((modes, 128), jnp.float32)] * 2,
        compiler_params=pltpu.CompilerParams(vmem_limit_bytes=VMEM_LIMIT),
    )(every, own, cross, omega_t)


def per_device(slabs, places, init_state, coef, source, amplitudes, sample_idx, step_counts, sketch_signs):
    _, snaps, rows, cols = init_state.shape
    signs = sketch_signs.astype(jnp.float32)
    omega_t = (2.0 * jnp.swapaxes(signs, 1, 2) - 1.0) / math.sqrt(sketch_signs.shape[1])
    parts = flow(slabs, places, init_state.reshape(snaps * rows, cols), coef[0], source,
                 amplitudes.reshape(1, -1), sample_idx, step_counts, omega_t)
    out = parts[0] if FUSED else merge(*parts, omega_t)
    modes = out.shape[1]
    return jnp.swapaxes(out, 0, 1).reshape(modes, rows, cols // places)


def solution(mesh):
    return jax.shard_map(
        functools.partial(per_device, mesh.shape["slab"], mesh.shape["param"]),
        mesh=mesh,
        in_specs=(
            P("param", None, "slab", None),
            P("param", "slab", None),
            P("slab", None),
            P(),
            P("param", None),
            P("param"),
            P(),
        ),
        out_specs=P(None, "slab", "param"),
        check_vma=False,
    )
```

```python
import functools
import math

import jax
import jax.numpy as jnp
from jax import lax
from jax.experimental import pallas as pl
from jax.experimental.pallas import tpu as pltpu
from jax.sharding import PartitionSpec as P

STEPS = 8
HALO = 4
BATCHES = 2
MESH = pl.DeviceIdType.MESH
HIGHEST = lax.Precision.HIGHEST
VMEM_LIMIT = 48 * 1024 * 1024
VMEM = pl.BlockSpec(memory_space=pltpu.VMEM)
SMEM = pl.BlockSpec(memory_space=pltpu.SMEM)


def dot(a, b):
    return lax.dot_general(a, b, (((1,), (0,)), ((), ())), precision=HIGHEST, preferred_element_type=jnp.float32)


def dot_t(a, b):
    return lax.dot_general(a, b, (((1,), (1,)), ((), ())), precision=HIGHEST, preferred_element_type=jnp.float32)


def flow_kernel(slabs, places, x_ref, coef_ref, source_ref, table_ref, idx_ref, count_ref, omega_ref, *refs):
    (every_ref, own_ref, cross_ref, buf, halo, stage, local, nearby, amp_ref, part, pieces, total, packed, fields, grams, mixes, tall, bits, mine, extra,
     out0, near_send, near_recv, halo_send, halo_recv, rs_send, rs_recv, ag_send, ag_recv, x_send, x_recv,
     g_send, g_recv, m_send, m_recv, rt_send, rt_recv, px_send, px_recv, at_send, at_recv) = refs
    rows, cols = coef_ref.shape
    snaps = part.shape[0]
    modes = omega_ref.shape[1]
    groups = rows // places
    count_pairs = places // 2
    share = snaps // slabs
    me = lax.axis_index("slab")
    place = lax.axis_index("param")
    peers = [lax.rem(me + k, slabs) for k in range(1, slabs)]

    barrier = pltpu.get_barrier_semaphore()
    for peer in peers:
        pl.semaphore_signal(barrier, inc=1, device_id=(place, peer), device_id_type=MESH)
    for k in range(1, places):
        pl.semaphore_signal(barrier, inc=1, device_id=(lax.rem(place + k, places), me), device_id_type=MESH)

    for r in range(rows):
        buf[0, HALO + r] = x_ref[pl.ds(r, snaps, stride=rows), :]

    table = jnp.broadcast_to(table_ref[...], (8, table_ref.shape[1]))
    entry = lax.broadcasted_iota(jnp.int32, (table_ref.shape[1], snaps), 0)
    picks = jnp.where(entry == idx_ref[...], 1.0, 0.0)
    amp_row = 0.1 * dot(table, picks)[0:1]
    amp_ref[...] = jnp.transpose(jnp.broadcast_to(amp_row, (cols, snaps)))

    half = snaps // BATCHES
    nothing = jnp.zeros((BATCHES, HALO, half, cols), jnp.float32)
    local[0] = coef_ref[...]
    local[1] = source_ref[...]

    @pl.when(me == 0)
    def _():
        nearby[0] = jnp.zeros((2, rows, cols), jnp.float32)
        for turn in range(STEPS // HALO):
            halo[turn, 0] = nothing

    @pl.when(me == slabs - 1)
    def _():
        nearby[1] = jnp.zeros((2, rows, cols), jnp.float32)
        for turn in range(STEPS // HALO):
            halo[turn, 1] = nothing

    pl.semaphore_wait(barrier, slabs + places - 2)
    after, before = lax.rem(me + 1, slabs), lax.rem(me + slabs - 1, slabs)

    def hand(src, dst, sems, target):
        return pltpu.make_async_remote_copy(
            src_ref=src, dst_ref=dst, send_sem=sems[0], recv_sem=sems[1],
            device_id=(place, target), device_id_type=MESH)

    def down(turn, b):
        return hand(stage.at[0, b], halo.at[turn, 0, b], (halo_send.at[turn, 0, b], halo_recv.at[turn, 0, b]), after)

    def up(turn, b):
        return hand(stage.at[1, b], halo.at[turn, 1, b], (halo_send.at[turn, 1, b], halo_recv.at[turn, 1, b]), before)

    def down_rates():
        return hand(local, nearby.at[0], (near_send.at[0], near_recv.at[0]), after)

    def up_rates():
        return hand(local, nearby.at[1], (near_send.at[1], near_recv.at[1]), before)

    def send(turn, b):
        now = turn * HALO % 2
        for h in range(HALO):
            stage[0, b, h] = buf[now, rows + h, pl.ds(b * half, half)]
            stage[1, b, h] = buf[now, HALO + h, pl.ds(b * half, half)]

        @pl.when(me < slabs - 1)
        def _():
            down(turn, b).start()
            if turn == 0 and b == 0:
                down_rates().start()

        @pl.when(me > 0)
        def _():
            up(turn, b).start()
            if turn == 0 and b == 0:
                up_rates().start()

    def settle(turn, b):
        @pl.when(me > 0)
        def _():
            down(turn, b).wait_recv()
            up(turn, b).wait_send()
            if turn == 0 and b == 0:
                down_rates().wait_recv()
                up_rates().wait_send()

        @pl.when(me < slabs - 1)
        def _():
            up(turn, b).wait_recv()
            down(turn, b).wait_send()
            if turn == 0 and b == 0:
                up_rates().wait_recv()
                down_rates().wait_send()

    count = count_ref[0]
    chunk = 32
    lane = lax.broadcasted_iota(jnp.int32, (chunk, cols), 1)
    first, last = lane == 0, lane == cols - 1

    def update(step, r, read, rates, spans):
        later = (step + 1) % 2
        active = jnp.where(step < count, 1.0, 0.0)
        rate = rates[0] * active
        half_rate = 0.5 * rate
        force = rates[1] * active
        for c in spans:
            s = pl.ds(c, chunk)
            f = read(r, s)
            left = jnp.where(first, 0.0, pltpu.roll(f, 1, 1))
            right = jnp.where(last, 0.0, pltpu.roll(f, cols - 1, 1))
            lap = read(r + 1, s) + read(r - 1, s) + right + left - 4.0 * f
            th = jnp.tanh(f)
            buf[later, HALO + r, s] = f + (rate + half_rate * (th * th)) * lap + amp_ref[s] * force

    def edge(step, r, b):
        turn, i = step // HALO, step % HALO

        def read(at, s):
            inside = pl.ds(s.start - b * half, s.size)
            if i == 0 and at < 0:
                return halo[turn, 0, b, HALO + at, inside]
            if i == 0 and at >= rows:
                return halo[turn, 1, b, at - rows, inside]
            return buf[step % 2, HALO + at, s]

        if r < 0:
            rates = [nearby[0, n, rows + r : rows + r + 1] for n in range(2)]
        elif r >= rows:
            rates = [nearby[1, n, r - rows : r - rows + 1] for n in range(2)]
        else:
            rates = [local[n, r : r + 1] for n in range(2)]
        update(step, r, read, rates, range(b * half, (b + 1) * half, chunk))

    for b in range(BATCHES):
        send(0, b)
    for turn in range(STEPS // HALO):
        for i in range(HALO):
            step = turn * HALO + i

            def inner(r, carry):
                update(step, r, lambda at, s: buf[step % 2, HALO + at, s], [local[n, pl.ds(r, 1)] for n in range(2)],
                       range(0, snaps, chunk))
                return carry

            lax.fori_loop(1 + i, rows - 1 - i, inner, 0)
        for b in range(BATCHES):
            settle(turn, b)
            for i in range(HALO):
                step = turn * HALO + i
                for r in list(range(i + 1 - HALO, 1 + i)) + list(range(rows - 1 - i, rows + HALO - 1 - i)):
                    edge(step, r, b)
            if turn < STEPS // HALO - 1:
                send(turn + 1, b)

    end = STEPS % 2

    width = cols // places
    slot = lax.broadcasted_iota(jnp.int32, (chunk, cols), 1) // width

    def pack(i, carry):
        group = i // (snaps // chunk)
        s = pl.ds(pl.multiple_of(i % (snaps // chunk) * chunk, chunk), chunk)
        parts = [buf[end, HALO + group * places + j, s] for j in range(places)]
        for q in range(places):
            whole = parts[q]
            for j in range(places):
                if j != q:
                    whole = jnp.where(slot == j, pltpu.roll(parts[j], (j - q) % places * width, 1), whole)
            packed[q, group, s] = whole
        return carry

    lax.fori_loop(0, groups * (snaps // chunk), pack, 0)

    def beside(k, src, dst, sems):
        return pltpu.make_async_remote_copy(
            src_ref=src, dst_ref=dst, send_sem=sems[0].at[k], recv_sem=sems[1].at[k],
            device_id=(lax.rem(place + k, places), me), device_id_type=MESH)

    def along(k, src, dst, sems):
        return pltpu.make_async_remote_copy(
            src_ref=src, dst_ref=dst, send_sem=sems[0].at[k], recv_sem=sems[1].at[k],
            device_id=(place, lax.rem(me + k, slabs)), device_id_type=MESH)

    def swap(k):
        return beside(k, packed.at[lax.rem(place + k, places)], fields.at[place], (x_send, x_recv))

    for k in range(1, places):
        swap(k).start()

    def products(i, acc):
        pair = jnp.concatenate([buf[end, HALO + 2 * i], buf[end, HALO + 2 * i + 1]], axis=1)
        return acc + dot_t(pair, pair)

    part[...] = lax.fori_loop(0, rows // 2, products, jnp.zeros((snaps, snaps), jnp.float32))

    def scatter(k):
        peer = lax.rem(me + k, slabs)
        return along(k, part.at[pl.ds(peer * share, share)], pieces.at[k], (rs_send, rs_recv))

    def gather(k):
        return along(k, total, grams.at[place, pl.ds(me * share, share)], (ag_send, ag_recv))

    for k in range(1, slabs):
        scatter(k).start()
    for group in range(groups):
        fields[place, group] = packed[place, group]
    acc = part[pl.ds(pl.multiple_of(me * share, 8), share)]
    for k in range(1, slabs):
        scatter(k).wait_recv()
        acc = acc + pieces[k]
    total[...] = acc
    for k in range(1, slabs):
        gather(k).start()
    grams[place, pl.ds(pl.multiple_of(me * share, 8), share)] = acc
    for k in range(1, slabs):
        gather(k).wait_recv()

    def lend(k):
        return beside(k, grams.at[place], grams.at[place], (g_send, g_recv))

    def share_mix(k):
        return beside(k, mixes.at[place], mixes.at[place], (m_send, m_recv))

    for k in range(1, places):
        lend(k).start()
    mixes[place] = mixings([grams[place]], omega_rows(omega_ref[0]), [out0])[0]
    for k in range(1, places):
        share_mix(k).start()
    for k in range(1, places):
        swap(k).wait_recv()
    for k in range(1, places):
        share_mix(k).wait_recv()
    for i in range(places):
        for group in range(groups):
            every_ref[i, group] = dot(mixes[i], fields[i, group])

    def piece(i):
        return jnp.concatenate([every_ref[i, g] for g in range(groups)], axis=1)

    def stacked(i):
        return jnp.concatenate([piece(2 * i), piece(2 * i + 1)], axis=0)

    at = 0
    for i in range(count_pairs):
        for j in range(i + 1, count_pairs):
            tall[at : at + 2 * modes] = dot_t(stacked(i), stacked(j))
            at += 2 * modes
    for i in range(0, count_pairs, 2):
        tall[at : at + modes] = jnp.concatenate(
            [dot_t(piece(2 * h), piece(2 * h + 1)) for h in (i, i + 1)], axis=1)
        at += modes
    span = at // slabs

    def scatter_tall(k):
        peer = lax.rem(me + k, slabs)
        return along(k, tall.at[pl.ds(peer * span, span)], bits.at[k], (rt_send, rt_recv))

    def across(k):
        return beside(k, extra.at[place], extra.at[place], (px_send, px_recv))

    def gather_tall(k):
        return along(k, mine, cross_ref.at[pl.ds(me * span, span)], (at_send, at_recv))

    for k in range(1, slabs):
        scatter_tall(k).start()
    for k in range(1, places):
        lend(k).wait_recv()
    for i in range(places):
        own_ref[i] = dot_t(dot(mixes[i], grams[i]), mixes[i])
    acc = tall[pl.ds(pl.multiple_of(me * span, 8), span)]
    for k in range(1, slabs):
        scatter_tall(k).wait_recv()
        acc = acc + bits[k]
    extra[place] = acc
    for k in range(1, places):
        across(k).start()
    for k in range(1, places):
        across(k).wait_recv()
    acc = extra[0]
    for k in range(1, places):
        acc = acc + extra[k]
    mine[...] = acc
    for k in range(1, slabs):
        gather_tall(k).start()
    cross_ref[pl.ds(pl.multiple_of(me * span, 8), span)] = acc
    for k in range(1, slabs):
        scatter(k).wait_send()
        gather(k).wait_send()
        scatter_tall(k).wait_send()
    for k in range(1, places):
        swap(k).wait_send()
        lend(k).wait_send()
        share_mix(k).wait_send()
        across(k).wait_send()
    for k in range(1, slabs):
        gather_tall(k).wait()

def flow(slabs, places, x, coef, source, table, idx, count, omega_t):
    rows, cols = coef.shape
    snaps = x.shape[0] // rows
    modes = omega_t.shape[1]
    groups = rows // places
    pairs = places // 2
    high = pairs * (pairs - 1) // 2 * 2 * modes + pairs // 2 * modes
    f32 = jnp.float32

    def sems(*shape):
        return [pltpu.SemaphoreType.DMA(shape)] * 2

    result = [(places, groups, modes, cols), (places, modes, modes), (high, 2 * modes)]
    return pl.pallas_call(
        functools.partial(flow_kernel, slabs, places),
        out_shape=[jax.ShapeDtypeStruct(shape, f32) for shape in result],
        in_specs=[VMEM, VMEM, VMEM, VMEM, VMEM, SMEM, VMEM],
        out_specs=[VMEM] * len(result),
        scratch_shapes=[
            pltpu.VMEM((2, rows + 2 * HALO, snaps, cols), f32),
            pltpu.VMEM((STEPS // HALO, 2, BATCHES, HALO, snaps // BATCHES, cols), f32),
            pltpu.VMEM((2, BATCHES, HALO, snaps // BATCHES, cols), f32),
            pltpu.VMEM((2, rows, cols), f32),
            pltpu.VMEM((2, 2, rows, cols), f32),
            pltpu.VMEM((snaps, cols), f32),
            pltpu.VMEM((snaps, snaps), f32),
            pltpu.VMEM((slabs, snaps // slabs, snaps), f32),
            pltpu.VMEM((snaps // slabs, snaps), f32),
            pltpu.VMEM((places, groups, snaps, cols), f32),
            pltpu.VMEM((places, groups, snaps, cols), f32),
            pltpu.VMEM((places, snaps, snaps), f32),
            pltpu.VMEM((places, modes, snaps), f32),
            pltpu.VMEM((high, 2 * modes), f32),
            pltpu.VMEM((slabs, high // slabs, 2 * modes), f32),
            pltpu.VMEM((high // slabs, 2 * modes), f32),
            pltpu.VMEM((places, high // slabs, 2 * modes), f32),
            pltpu.VMEM((modes, 128), f32),
        ] + sems(2) + sems(STEPS // HALO, 2, BATCHES) + 2 * sems(slabs) + 3 * sems(places)
        + sems(slabs) + sems(places) + sems(slabs),
        compiler_params=pltpu.CompilerParams(collective_id=0, has_side_effects=True, vmem_limit_bytes=VMEM_LIMIT),
    )(x, coef, source, table, idx, count, omega_t)


def eliminate(problems, outs):
    size = problems[0][0].shape[0]
    blocks = size // 8
    wide = 128
    sub = lax.broadcasted_iota(jnp.int32, (8, wide), 0)

    def split(value):
        return tuple(value[8 * b : 8 * b + 8] for b in range(blocks))

    def padded(m):
        return jnp.concatenate([m, jnp.zeros((size, wide - size), jnp.float32)], axis=1)

    start = tuple((split(padded(m)), split(r)) for m, r in problems)

    def spread(value, k):
        return jnp.broadcast_to(value[k : k + 1], (8, wide))

    def body(t, carry):
        states = []
        for ms, rs in carry:
            cols = [jnp.broadcast_to(ms[0][:, k : k + 1], (8, wide)) for k in range(8)]
            zero = jnp.zeros((8, wide), jnp.float32)
            states.append([ms[0], rs[0], cols, zero, zero])
        for k in range(8):
            for state in states:
                m0, r0, cols, done, scale = state
                pivot = spread(cols[k], k)
                inv = 1.0 / pivot
                factor = jnp.where(sub == k, 0.0, cols[k] * inv)
                done = jnp.where(sub == k, r0 * lax.rsqrt(pivot), done)
                scale = jnp.where(sub == k, inv, scale)
                cols = [c if j <= k else c - factor * spread(c, k) for j, c in enumerate(cols)]
                state[:] = [m0 - factor * spread(m0, k), r0 - factor * spread(r0, k), cols, done, scale]
        following = []
        for (ms, rs), (m0, r0, _, done, scale), out in zip(carry, states, outs):
            out[pl.ds(pl.multiple_of(8 * t, 8), 8), :] = done
            rows_m = [spread(m0 * scale, k) for k in range(8)]
            rows_r = [spread(r0 * scale, k) for k in range(8)]
            next_m, next_r = [], []
            for m, r in zip(ms[1:], rs[1:]):
                less_m = less_r = 0.0
                for k in range(8):
                    col = jnp.broadcast_to(m[:, k : k + 1], (8, wide))
                    less_m, less_r = less_m + col * rows_m[k], less_r + col * rows_r[k]
                next_m.append(pltpu.roll(m - less_m, wide - 8, 1))
                next_r.append(r - less_r)
            zero = jnp.zeros((8, wide), jnp.float32)
            following.append((tuple(next_m + [zero]), tuple(next_r + [zero])))
        return tuple(following)

    lax.fori_loop(0, blocks, body, start)


def omega_rows(signs):
    return (2.0 * signs.astype(jnp.float32) - 1.0) / math.sqrt(signs.shape[1])


def shifted(m):
    size = m.shape[0]
    eye = lax.broadcasted_iota(jnp.int32, m.shape, 0) == lax.broadcasted_iota(jnp.int32, m.shape, 1)
    trace = jnp.sum(jnp.where(eye, m, 0.0), keepdims=True)
    return m + jnp.where(eye, (0.0001 / size) * trace, 0.0)


def mixings(grams, omega_t, outs):
    size = omega_t.shape[0]
    moments = [shifted(dot_t(dot(omega_t, g), omega_t)) for g in grams]
    eliminate([(m, omega_t) for m in moments], outs)
    lefts = [out[...] for out in outs[: len(grams)]]
    inners = []
    for left, g in zip(lefts, grams):
        hmat = dot(left, g)
        inners.append(shifted(dot_t(hmat, hmat)))
    pad = jnp.zeros((size, 128 - size), jnp.float32)
    eliminate([(c, jnp.concatenate([c, pad], axis=1)) for c in inners], outs)
    return [dot(out[:, :size], left) for out, left in zip(outs, lefts)]


def merge_levels(every_ref, own_ref, cross_ref, omega_ref, modes_ref, *outs):
    places, groups, modes, cols = every_ref.shape
    size = 2 * modes
    width = cols // places
    count = places // 2
    blocks = {}
    at = 0
    for i in range(count):
        for j in range(i + 1, count):
            blocks[i, j] = cross_ref[at : at + size]
            at += size
    for i in range(0, count, 2):
        both = cross_ref[at : at + modes]
        at += modes
        for h in range(2):
            inner = both[:, h * modes : (h + 1) * modes]
            top = jnp.concatenate([own_ref[2 * (i + h)], inner], axis=1)
            bottom = jnp.concatenate([jnp.transpose(inner), own_ref[2 * (i + h) + 1]], axis=1)
            blocks[i + h, i + h] = jnp.concatenate([top, bottom], axis=0)
    trees = None
    level = 0
    while count:
        mixes = []
        for at in range(0, count, 2):
            some = range(at, min(at + 2, count))
            mixes += mixings([0.5 * blocks[i, i] for i in some], omega_rows(omega_ref[level + 1]), outs)
        mixes = [0.5**0.5 * m for m in mixes]
        if trees is None:
            trees = mixes
        else:
            trees = [
                jnp.concatenate([dot(m[:, :modes], trees[2 * i]), dot(m[:, modes:], trees[2 * i + 1])], axis=1)
                for i, m in enumerate(mixes)
            ]
        count //= 2
        level += 1
        if count:
            fine = {}
            for i in range(2 * count):
                for j in range(i, 2 * count):
                    fine[i, j] = dot_t(dot(mixes[i], blocks[i, j]), mixes[j])
            blocks = {}
            for i in range(count):
                for j in range(i, count):
                    lower = fine[2 * i + 1, 2 * j] if i < j else jnp.transpose(fine[2 * i, 2 * j + 1])
                    top = jnp.concatenate([fine[2 * i, 2 * j], fine[2 * i, 2 * j + 1]], axis=1)
                    bottom = jnp.concatenate([lower, fine[2 * i + 1, 2 * j + 1]], axis=1)
                    blocks[i, j] = jnp.concatenate([top, bottom], axis=0)
    tree = trees[0]
    for group in range(groups):
        stacked = jnp.concatenate([every_ref[i, group] for i in range(places)], axis=0)
        whole = jnp.transpose(dot(tree, stacked))
        for j in range(places):
            modes_ref[group * places + j] = whole[j * width : (j + 1) * width]


def merge(every, own, cross, omega_t):
    places, groups, modes, cols = every.shape
    return pl.pallas_call(
        merge_levels,
        out_shape=jax.ShapeDtypeStruct((groups * places, cols // places, modes), jnp.float32),
        in_specs=[VMEM] * 4,
        out_specs=VMEM,
        scratch_shapes=[pltpu.VMEM((modes, 128), jnp.float32)] * 2,
        compiler_params=pltpu.CompilerParams(vmem_limit_bytes=VMEM_LIMIT),
    )(every, own, cross, omega_t)


def per_device(slabs, places, init_state, coef, source, amplitudes, sample_idx, step_counts, sketch_signs):
    _, snaps, rows, cols = init_state.shape
    signs = jnp.swapaxes(sketch_signs, 1, 2)
    parts = flow(slabs, places, init_state.reshape(snaps * rows, cols), coef[0], source,
                 amplitudes.reshape(1, -1), sample_idx, step_counts, signs)
    out = merge(*parts, signs)
    return jnp.transpose(out, (2, 0, 1))


def solution(mesh):
    return jax.shard_map(
        functools.partial(per_device, mesh.shape["slab"], mesh.shape["param"]),
        mesh=mesh,
        in_specs=(
            P("param", None, "slab", None),
            P("param", "slab", None),
            P("slab", None),
            P(),
            P("param", None),
            P("param"),
            P(),
        ),
        out_specs=P(None, "slab", "param"),
        check_vma=False,
    )
```

```python
import functools
import math

import jax
import jax.numpy as jnp
from jax import lax
from jax.experimental import pallas as pl
from jax.experimental.pallas import tpu as pltpu
from jax.sharding import PartitionSpec as P

STEPS = 8
HALO = 2
BATCHES = 2
MESH = pl.DeviceIdType.MESH
HIGHEST = lax.Precision.HIGHEST
VMEM_LIMIT = 63 * 1024 * 1024
VMEM = pl.BlockSpec(memory_space=pltpu.VMEM)
HBM = pl.BlockSpec(memory_space=pltpu.HBM)
SMEM = pl.BlockSpec(memory_space=pltpu.SMEM)


def dot(a, b):
    return lax.dot_general(a, b, (((1,), (0,)), ((), ())), precision=HIGHEST, preferred_element_type=jnp.float32)


def dot_t(a, b):
    return lax.dot_general(a, b, (((1,), (1,)), ((), ())), precision=HIGHEST, preferred_element_type=jnp.float32)


def flow_kernel(slabs, places, x_far, coef_ref, source_far, table_far, idx_far, count_ref, signs_far, *refs):
    (every_ref, own_ref, cross_ref, x_ref, table_ref, idx_ref, signs_ref, load_sem, buf, halo, stage, local, nearby, amp_ref, part, pieces, total, packed, fields, grams, mixes, tall, bits, mine, extra,
     out0, near_send, near_recv, halo_send, halo_recv, rs_send, rs_recv, ag_send, ag_recv, x_send, x_recv,
     g_send, g_recv, m_send, m_recv, rt_send, rt_recv, px_send, px_recv, at_send, at_recv) = refs
    rows, cols = coef_ref.shape
    snaps = part.shape[0]
    modes = signs_ref.shape[0]
    groups = rows // places
    count_pairs = places // 2
    share = snaps // slabs
    me = lax.axis_index("slab")
    place = lax.axis_index("param")
    peers = [lax.rem(me + k, slabs) for k in range(1, slabs)]

    loads = [
        pltpu.make_async_copy(src, dst, load_sem.at[n])
        for n, (src, dst) in enumerate([
            (x_far, x_ref), (coef_ref, local.at[0]), (source_far, local.at[1]),
            (table_far, table_ref), (idx_far, idx_ref), (signs_far.at[0], signs_ref)])
    ]
    for load in loads:
        load.start()

    barrier = pltpu.get_barrier_semaphore()
    for peer in peers:
        pl.semaphore_signal(barrier, inc=1, device_id=(place, peer), device_id_type=MESH)
    for k in range(1, places):
        pl.semaphore_signal(barrier, inc=1, device_id=(lax.rem(place + k, places), me), device_id_type=MESH)

    for load in loads:
        load.wait()
    for r in range(rows):
        buf[0, HALO + r] = x_ref[pl.ds(r, snaps, stride=rows), :]

    table = jnp.broadcast_to(table_ref[...], (8, table_ref.shape[1]))
    entry = lax.broadcasted_iota(jnp.int32, (table_ref.shape[1], snaps), 0)
    picks = jnp.where(entry == idx_ref[...], 1.0, 0.0)
    amp_row = 0.1 * dot(table, picks)[0:1]
    amp_ref[...] = jnp.transpose(jnp.broadcast_to(amp_row, (cols, snaps)))

    half = snaps // BATCHES
    nothing = jnp.zeros((BATCHES, HALO, half, cols), jnp.float32)

    @pl.when(me == 0)
    def _():
        nearby[0] = jnp.zeros((2, rows, cols), jnp.float32)
        for turn in range(STEPS // HALO):
            halo[turn, 0] = nothing

    @pl.when(me == slabs - 1)
    def _():
        nearby[1] = jnp.zeros((2, rows, cols), jnp.float32)
        for turn in range(STEPS // HALO):
            halo[turn, 1] = nothing

    pl.semaphore_wait(barrier, slabs + places - 2)
    after, before = lax.rem(me + 1, slabs), lax.rem(me + slabs - 1, slabs)

    def hand(src, dst, sems, target):
        return pltpu.make_async_remote_copy(
            src_ref=src, dst_ref=dst, send_sem=sems[0], recv_sem=sems[1],
            device_id=(place, target), device_id_type=MESH)

    def down(turn, b):
        return hand(stage.at[0, b], halo.at[turn, 0, b], (halo_send.at[turn, 0, b], halo_recv.at[turn, 0, b]), after)

    def up(turn, b):
        return hand(stage.at[1, b], halo.at[turn, 1, b], (halo_send.at[turn, 1, b], halo_recv.at[turn, 1, b]), before)

    def down_rates():
        return hand(local, nearby.at[0], (near_send.at[0], near_recv.at[0]), after)

    def up_rates():
        return hand(local, nearby.at[1], (near_send.at[1], near_recv.at[1]), before)

    def send(turn, b):
        now = turn * HALO % 2
        for h in range(HALO):
            stage[0, b, h] = buf[now, rows + h, pl.ds(b * half, half)]
            stage[1, b, h] = buf[now, HALO + h, pl.ds(b * half, half)]

        @pl.when(me < slabs - 1)
        def _():
            down(turn, b).start()
            if turn == 0 and b == 0:
                down_rates().start()

        @pl.when(me > 0)
        def _():
            up(turn, b).start()
            if turn == 0 and b == 0:
                up_rates().start()

    def settle(turn, b):
        @pl.when(me > 0)
        def _():
            down(turn, b).wait_recv()
            up(turn, b).wait_send()
            if turn == 0 and b == 0:
                down_rates().wait_recv()
                up_rates().wait_send()

        @pl.when(me < slabs - 1)
        def _():
            up(turn, b).wait_recv()
            down(turn, b).wait_send()
            if turn == 0 and b == 0:
                up_rates().wait_recv()
                down_rates().wait_send()

    count = count_ref[0]
    chunk = 32
    lane = lax.broadcasted_iota(jnp.int32, (chunk, cols), 1)
    first, last = lane == 0, lane == cols - 1

    def update(step, r, read, rates, spans):
        later = (step + 1) % 2
        active = jnp.where(step < count, 1.0, 0.0)
        rate = rates[0] * active
        half_rate = 0.5 * rate
        force = rates[1] * active
        for c in spans:
            s = pl.ds(c, chunk)
            f = read(r, s)
            left = jnp.where(first, 0.0, pltpu.roll(f, 1, 1))
            right = jnp.where(last, 0.0, pltpu.roll(f, cols - 1, 1))
            lap = read(r + 1, s) + read(r - 1, s) + right + left - 4.0 * f
            th = jnp.tanh(f)
            buf[later, HALO + r, s] = f + (rate + half_rate * (th * th)) * lap + amp_ref[s] * force

    def edge(step, r, b):
        turn, i = step // HALO, step % HALO

        def read(at, s):
            inside = pl.ds(s.start - b * half, s.size)
            if i == 0 and at < 0:
                return halo[turn, 0, b, HALO + at, inside]
            if i == 0 and at >= rows:
                return halo[turn, 1, b, at - rows, inside]
            return buf[step % 2, HALO + at, s]

        if r < 0:
            rates = [nearby[0, n, rows + r : rows + r + 1] for n in range(2)]
        elif r >= rows:
            rates = [nearby[1, n, r - rows : r - rows + 1] for n in range(2)]
        else:
            rates = [local[n, r : r + 1] for n in range(2)]
        update(step, r, read, rates, range(b * half, (b + 1) * half, chunk))

    for b in range(BATCHES):
        send(0, b)
    for turn in range(STEPS // HALO):
        for i in range(HALO):
            step = turn * HALO + i

            def inner(r, carry):
                update(step, r, lambda at, s: buf[step % 2, HALO + at, s], [local[n, pl.ds(r, 1)] for n in range(2)],
                       range(0, snaps, chunk))
                return carry

            lax.fori_loop(1 + i, rows - 1 - i, inner, 0)
        for b in range(BATCHES):
            settle(turn, b)
            for i in range(HALO):
                step = turn * HALO + i
                for r in list(range(i + 1 - HALO, 1 + i)) + list(range(rows - 1 - i, rows + HALO - 1 - i)):
                    edge(step, r, b)
            if turn < STEPS // HALO - 1:
                send(turn + 1, b)

    end = STEPS % 2

    width = cols // places
    slot = lax.broadcasted_iota(jnp.int32, (chunk, cols), 1) // width

    def pack(i, carry):
        group = i // (snaps // chunk)
        s = pl.ds(pl.multiple_of(i % (snaps // chunk) * chunk, chunk), chunk)
        parts = [buf[end, HALO + group * places + j, s] for j in range(places)]
        for q in range(places):
            whole = parts[q]
            for j in range(places):
                if j != q:
                    whole = jnp.where(slot == j, pltpu.roll(parts[j], (j - q) % places * width, 1), whole)
            packed[q, group, s] = whole
        return carry

    lax.fori_loop(0, groups * (snaps // chunk), pack, 0)

    def beside(k, src, dst, sems):
        return pltpu.make_async_remote_copy(
            src_ref=src, dst_ref=dst, send_sem=sems[0].at[k], recv_sem=sems[1].at[k],
            device_id=(lax.rem(place + k, places), me), device_id_type=MESH)

    def along(k, src, dst, sems):
        return pltpu.make_async_remote_copy(
            src_ref=src, dst_ref=dst, send_sem=sems[0].at[k], recv_sem=sems[1].at[k],
            device_id=(place, lax.rem(me + k, slabs)), device_id_type=MESH)

    def swap(k):
        return beside(k, packed.at[lax.rem(place + k, places)], fields.at[place], (x_send, x_recv))

    for k in range(1, places):
        swap(k).start()

    def products(i, acc):
        pair = jnp.concatenate([buf[end, HALO + 2 * i], buf[end, HALO + 2 * i + 1]], axis=1)
        return acc + dot_t(pair, pair)

    part[...] = lax.fori_loop(0, rows // 2, products, jnp.zeros((snaps, snaps), jnp.float32))

    def scatter(k):
        peer = lax.rem(me + k, slabs)
        return along(k, part.at[pl.ds(peer * share, share)], pieces.at[k], (rs_send, rs_recv))

    def gather(k):
        return along(k, total, grams.at[place, pl.ds(me * share, share)], (ag_send, ag_recv))

    for k in range(1, slabs):
        scatter(k).start()
    for group in range(groups):
        fields[place, group] = packed[place, group]
    acc = part[pl.ds(pl.multiple_of(me * share, 8), share)]
    for k in range(1, slabs):
        scatter(k).wait_recv()
        acc = acc + pieces[k]
    total[...] = acc
    for k in range(1, slabs):
        gather(k).start()
    grams[place, pl.ds(pl.multiple_of(me * share, 8), share)] = acc
    for k in range(1, slabs):
        gather(k).wait_recv()

    def lend(k):
        return beside(k, grams.at[place], grams.at[place], (g_send, g_recv))

    def share_mix(k):
        return beside(k, mixes.at[place], mixes.at[place], (m_send, m_recv))

    for k in range(1, places):
        lend(k).start()
    mixes[place] = mixings([grams[place]], omega_rows(signs_ref[...]), [out0])[0]
    for k in range(1, places):
        share_mix(k).start()
    for k in range(1, places):
        swap(k).wait_recv()
    for k in range(1, places):
        share_mix(k).wait_recv()
    for i in range(places):
        for group in range(groups):
            every_ref[i, group] = dot(mixes[i], fields[i, group])

    def piece(i):
        return jnp.concatenate([every_ref[i, g] for g in range(groups)], axis=1)

    def stacked(i):
        return jnp.concatenate([piece(2 * i), piece(2 * i + 1)], axis=0)

    at = 0
    for i in range(count_pairs):
        for j in range(i + 1, count_pairs):
            tall[at : at + 2 * modes] = dot_t(stacked(i), stacked(j))
            at += 2 * modes
    for i in range(0, count_pairs, 2):
        tall[at : at + modes] = jnp.concatenate(
            [dot_t(piece(2 * h), piece(2 * h + 1)) for h in (i, i + 1)], axis=1)
        at += modes
    span = at // slabs

    def scatter_tall(k):
        peer = lax.rem(me + k, slabs)
        return along(k, tall.at[pl.ds(peer * span, span)], bits.at[k], (rt_send, rt_recv))

    def across(k):
        return beside(k, extra.at[place], extra.at[place], (px_send, px_recv))

    def gather_tall(k):
        return along(k, mine, cross_ref.at[pl.ds(me * span, span)], (at_send, at_recv))

    for k in range(1, slabs):
        scatter_tall(k).start()
    for k in range(1, places):
        lend(k).wait_recv()
    for i in range(places):
        own_ref[i] = dot_t(dot(mixes[i], grams[i]), mixes[i])
    acc = tall[pl.ds(pl.multiple_of(me * span, 8), span)]
    for k in range(1, slabs):
        scatter_tall(k).wait_recv()
        acc = acc + bits[k]
    extra[place] = acc
    for k in range(1, places):
        across(k).start()
    for k in range(1, places):
        across(k).wait_recv()
    acc = extra[0]
    for k in range(1, places):
        acc = acc + extra[k]
    mine[...] = acc
    for k in range(1, slabs):
        gather_tall(k).start()
    cross_ref[pl.ds(pl.multiple_of(me * span, 8), span)] = acc
    for k in range(1, slabs):
        scatter(k).wait_send()
        gather(k).wait_send()
        scatter_tall(k).wait_send()
    for k in range(1, places):
        swap(k).wait_send()
        lend(k).wait_send()
        share_mix(k).wait_send()
        across(k).wait_send()
    for k in range(1, slabs):
        gather_tall(k).wait()

def flow(slabs, places, x, coef, source, table, idx, count, omega_t):
    rows, cols = coef.shape
    snaps = x.shape[0] // rows
    modes = omega_t.shape[1]
    groups = rows // places
    pairs = places // 2
    high = pairs * (pairs - 1) // 2 * 2 * modes + pairs // 2 * modes
    f32 = jnp.float32

    def sems(*shape):
        return [pltpu.SemaphoreType.DMA(shape)] * 2

    result = [(places, groups, modes, cols), (places, modes, modes), (high, 2 * modes)]
    return pl.pallas_call(
        functools.partial(flow_kernel, slabs, places),
        out_shape=[jax.ShapeDtypeStruct(shape, f32) for shape in result],
        in_specs=[HBM, HBM, HBM, HBM, HBM, SMEM, HBM],
        out_specs=[VMEM] * len(result),
        scratch_shapes=[
            pltpu.VMEM(x.shape, f32),
            pltpu.VMEM(table.shape, f32),
            pltpu.VMEM(idx.shape, jnp.int32),
            pltpu.VMEM(omega_t.shape[1:], jnp.int32),
            pltpu.SemaphoreType.DMA((6,)),
            pltpu.VMEM((2, rows + 2 * HALO, snaps, cols), f32),
            pltpu.VMEM((STEPS // HALO, 2, BATCHES, HALO, snaps // BATCHES, cols), f32),
            pltpu.VMEM((2, BATCHES, HALO, snaps // BATCHES, cols), f32),
            pltpu.VMEM((2, rows, cols), f32),
            pltpu.VMEM((2, 2, rows, cols), f32),
            pltpu.VMEM((snaps, cols), f32),
            pltpu.VMEM((snaps, snaps), f32),
            pltpu.VMEM((slabs, snaps // slabs, snaps), f32),
            pltpu.VMEM((snaps // slabs, snaps), f32),
            pltpu.VMEM((places, groups, snaps, cols), f32),
            pltpu.VMEM((places, groups, snaps, cols), f32),
            pltpu.VMEM((places, snaps, snaps), f32),
            pltpu.VMEM((places, modes, snaps), f32),
            pltpu.VMEM((high, 2 * modes), f32),
            pltpu.VMEM((slabs, high // slabs, 2 * modes), f32),
            pltpu.VMEM((high // slabs, 2 * modes), f32),
            pltpu.VMEM((places, high // slabs, 2 * modes), f32),
            pltpu.VMEM((modes, 128), f32),
        ] + sems(2) + sems(STEPS // HALO, 2, BATCHES) + 2 * sems(slabs) + 3 * sems(places)
        + sems(slabs) + sems(places) + sems(slabs),
        compiler_params=pltpu.CompilerParams(collective_id=0, has_side_effects=True, vmem_limit_bytes=VMEM_LIMIT),
    )(x, coef, source, table, idx, count, omega_t)


def eliminate(problems, outs):
    size = problems[0][0].shape[0]
    blocks = size // 8
    wide = 128
    sub = lax.broadcasted_iota(jnp.int32, (8, wide), 0)

    def split(value):
        return tuple(value[8 * b : 8 * b + 8] for b in range(blocks))

    def padded(m):
        return jnp.concatenate([m, jnp.zeros((size, wide - size), jnp.float32)], axis=1)

    start = tuple((split(padded(m)), split(r)) for m, r in problems)

    def spread(value, k):
        return jnp.broadcast_to(value[k : k + 1], (8, wide))

    def body(t, carry):
        states = []
        for ms, rs in carry:
            cols = [jnp.broadcast_to(ms[0][:, k : k + 1], (8, wide)) for k in range(8)]
            zero = jnp.zeros((8, wide), jnp.float32)
            states.append([ms[0], rs[0], cols, zero, zero, spread(cols[0], 0)])
        for k in range(8):
            for state in states:
                m0, r0, cols, done, scale, pivot = state
                inv = 1.0 / pivot
                done = jnp.where(sub == k, r0 * lax.rsqrt(pivot), done)
                scale = jnp.where(sub == k, inv, scale)
                hidden = jnp.where(sub == k, 0.0, cols[k])
                heads = [spread(c, k) if j > k else None for j, c in enumerate(cols)]
                if k < 7:
                    pivot = spread(cols[k + 1], k + 1) - spread(cols[k], k + 1) * heads[k + 1] * inv
                cols = [c if j <= k else c - hidden * heads[j] * inv for j, c in enumerate(cols)]
                m0 = m0 - hidden * spread(m0, k) * inv
                r0 = r0 - hidden * spread(r0, k) * inv
                state[:] = [m0, r0, cols, done, scale, pivot]
        following = []
        for (ms, rs), (m0, r0, _, done, scale, _), out in zip(carry, states, outs):
            out[pl.ds(pl.multiple_of(8 * t, 8), 8), :] = done
            rows_m = [spread(m0 * scale, k) for k in range(8)]
            rows_r = [spread(r0 * scale, k) for k in range(8)]
            next_m, next_r = [], []
            for m, r in zip(ms[1:], rs[1:]):
                less_m = less_r = 0.0
                for k in range(8):
                    col = jnp.broadcast_to(m[:, k : k + 1], (8, wide))
                    less_m, less_r = less_m + col * rows_m[k], less_r + col * rows_r[k]
                next_m.append(pltpu.roll(m - less_m, wide - 8, 1))
                next_r.append(r - less_r)
            zero = jnp.zeros((8, wide), jnp.float32)
            following.append((tuple(next_m + [zero]), tuple(next_r + [zero])))
        return tuple(following)

    lax.fori_loop(0, blocks, body, start)


def omega_rows(signs):
    return (2.0 * signs.astype(jnp.float32) - 1.0) / math.sqrt(signs.shape[1])


def shifted(m):
    size = m.shape[0]
    eye = lax.broadcasted_iota(jnp.int32, m.shape, 0) == lax.broadcasted_iota(jnp.int32, m.shape, 1)
    trace = jnp.sum(jnp.where(eye, m, 0.0), keepdims=True)
    return m + jnp.where(eye, (0.0001 / size) * trace, 0.0)


def mixings(grams, omega_t, outs):
    size = omega_t.shape[0]
    moments = [shifted(dot_t(dot(omega_t, g), omega_t)) for g in grams]
    eliminate([(m, omega_t) for m in moments], outs)
    lefts = [out[...] for out in outs[: len(grams)]]
    inners = []
    for left, g in zip(lefts, grams):
        hmat = dot(left, g)
        inners.append(shifted(dot_t(hmat, hmat)))
    pad = jnp.zeros((size, 128 - size), jnp.float32)
    eliminate([(c, jnp.concatenate([c, pad], axis=1)) for c in inners], outs)
    return [dot(out[:, :size], left) for out, left in zip(outs, lefts)]


def merge_levels(every_ref, own_ref, cross_ref, omega_ref, modes_ref, *outs):
    places, groups, modes, cols = every_ref.shape
    size = 2 * modes
    width = cols // places
    count = places // 2
    blocks = {}
    at = 0
    for i in range(count):
        for j in range(i + 1, count):
            blocks[i, j] = cross_ref[at : at + size]
            at += size
    for i in range(0, count, 2):
        both = cross_ref[at : at + modes]
        at += modes
        for h in range(2):
            inner = both[:, h * modes : (h + 1) * modes]
            top = jnp.concatenate([own_ref[2 * (i + h)], inner], axis=1)
            bottom = jnp.concatenate([jnp.transpose(inner), own_ref[2 * (i + h) + 1]], axis=1)
            blocks[i + h, i + h] = jnp.concatenate([top, bottom], axis=0)
    trees = None
    level = 0
    while count:
        mixes = []
        for at in range(0, count, 2):
            some = range(at, min(at + 2, count))
            mixes += mixings([0.5 * blocks[i, i] for i in some], omega_rows(omega_ref[level + 1]), outs)
        mixes = [0.5**0.5 * m for m in mixes]
        if trees is None:
            trees = mixes
        else:
            trees = [
                jnp.concatenate([dot(m[:, :modes], trees[2 * i]), dot(m[:, modes:], trees[2 * i + 1])], axis=1)
                for i, m in enumerate(mixes)
            ]
        count //= 2
        level += 1
        if count:
            fine = {}
            for i in range(2 * count):
                for j in range(i, 2 * count):
                    fine[i, j] = dot_t(dot(mixes[i], blocks[i, j]), mixes[j])
            blocks = {}
            for i in range(count):
                for j in range(i, count):
                    lower = fine[2 * i + 1, 2 * j] if i < j else jnp.transpose(fine[2 * i, 2 * j + 1])
                    top = jnp.concatenate([fine[2 * i, 2 * j], fine[2 * i, 2 * j + 1]], axis=1)
                    bottom = jnp.concatenate([lower, fine[2 * i + 1, 2 * j + 1]], axis=1)
                    blocks[i, j] = jnp.concatenate([top, bottom], axis=0)
    tree = trees[0]
    for group in range(groups):
        stacked = jnp.concatenate([every_ref[i, group] for i in range(places)], axis=0)
        whole = jnp.transpose(dot(tree, stacked))
        for j in range(places):
            modes_ref[group * places + j] = whole[j * width : (j + 1) * width]


def merge(every, own, cross, omega_t):
    places, groups, modes, cols = every.shape
    return pl.pallas_call(
        merge_levels,
        out_shape=jax.ShapeDtypeStruct((groups * places, cols // places, modes), jnp.float32),
        in_specs=[VMEM] * 4,
        out_specs=VMEM,
        scratch_shapes=[pltpu.VMEM((modes, 128), jnp.float32)] * 2,
        compiler_params=pltpu.CompilerParams(vmem_limit_bytes=VMEM_LIMIT),
    )(every, own, cross, omega_t)


def per_device(slabs, places, init_state, coef, source, amplitudes, sample_idx, step_counts, sketch_signs):
    _, snaps, rows, cols = init_state.shape
    signs = jnp.swapaxes(sketch_signs, 1, 2)
    parts = flow(slabs, places, init_state.reshape(snaps * rows, cols), coef[0], source,
                 amplitudes.reshape(1, -1), sample_idx, step_counts, signs)
    out = merge(*parts, signs)
    return jnp.transpose(out, (2, 0, 1))


def solution(mesh):
    return jax.shard_map(
        functools.partial(per_device, mesh.shape["slab"], mesh.shape["param"]),
        mesh=mesh,
        in_specs=(
            P("param", None, "slab", None),
            P("param", "slab", None),
            P("slab", None),
            P(),
            P("param", None),
            P("param"),
            P(),
        ),
        out_specs=P(None, "slab", "param"),
        check_vma=False,
    )
```

```python
import functools
import math

import jax
import jax.numpy as jnp
from jax import lax
from jax.experimental import pallas as pl
from jax.experimental.pallas import tpu as pltpu
from jax.sharding import PartitionSpec as P

STEPS = 8
HALO = 2
BATCHES = 2
MESH = pl.DeviceIdType.MESH
HIGHEST = lax.Precision.HIGHEST
VMEM_LIMIT = 63 * 1024 * 1024
VMEM = pl.BlockSpec(memory_space=pltpu.VMEM)
HBM = pl.BlockSpec(memory_space=pltpu.HBM)
SMEM = pl.BlockSpec(memory_space=pltpu.SMEM)


def dot(a, b):
    return lax.dot_general(a, b, (((1,), (0,)), ((), ())), precision=HIGHEST, preferred_element_type=jnp.float32)


def dot_t(a, b):
    return lax.dot_general(a, b, (((1,), (1,)), ((), ())), precision=HIGHEST, preferred_element_type=jnp.float32)


def flow_kernel(slabs, places, x_far, coef_ref, source_far, table_far, idx_far, count_ref, signs_far, *refs):
    (modes_ref, every_ref, own_ref, cross_ref, x_ref, table_ref, idx_ref, signs_ref, load_sem, buf, halo, stage, local, nearby, amp_ref, part, pieces, total, packed, fields, grams, mixes, tall, bits, mine, extra,
     out0, out1, near_send, near_recv, halo_send, halo_recv, rs_send, rs_recv, ag_send, ag_recv, x_send, x_recv,
     g_send, g_recv, m_send, m_recv, rt_send, rt_recv, px_send, px_recv, at_send, at_recv) = refs
    rows, cols = coef_ref.shape
    snaps = part.shape[0]
    modes = signs_ref.shape[1]
    groups = rows // places
    count_pairs = places // 2
    share = snaps // slabs
    me = lax.axis_index("slab")
    place = lax.axis_index("param")
    peers = [lax.rem(me + k, slabs) for k in range(1, slabs)]

    loads = [
        pltpu.make_async_copy(src, dst, load_sem.at[n])
        for n, (src, dst) in enumerate([
            (x_far, x_ref), (coef_ref, local.at[0]), (source_far, local.at[1]),
            (table_far, table_ref), (idx_far, idx_ref), (signs_far, signs_ref)])
    ]
    for load in loads:
        load.start()

    barrier = pltpu.get_barrier_semaphore()
    for peer in peers:
        pl.semaphore_signal(barrier, inc=1, device_id=(place, peer), device_id_type=MESH)
    for k in range(1, places):
        pl.semaphore_signal(barrier, inc=1, device_id=(lax.rem(place + k, places), me), device_id_type=MESH)

    for load in loads:
        load.wait()
    for r in range(rows):
        buf[0, HALO + r] = x_ref[pl.ds(r, snaps, stride=rows), :]

    table = jnp.broadcast_to(table_ref[...], (8, table_ref.shape[1]))
    entry = lax.broadcasted_iota(jnp.int32, (table_ref.shape[1], snaps), 0)
    picks = jnp.where(entry == idx_ref[...], 1.0, 0.0)
    amp_row = 0.1 * dot(table, picks)[0:1]
    amp_ref[...] = jnp.transpose(jnp.broadcast_to(amp_row, (cols, snaps)))

    half = snaps // BATCHES
    nothing = jnp.zeros((BATCHES, HALO, half, cols), jnp.float32)

    @pl.when(me == 0)
    def _():
        nearby[0] = jnp.zeros((2, rows, cols), jnp.float32)
        for turn in range(STEPS // HALO):
            halo[turn, 0] = nothing

    @pl.when(me == slabs - 1)
    def _():
        nearby[1] = jnp.zeros((2, rows, cols), jnp.float32)
        for turn in range(STEPS // HALO):
            halo[turn, 1] = nothing

    pl.semaphore_wait(barrier, slabs + places - 2)
    after, before = lax.rem(me + 1, slabs), lax.rem(me + slabs - 1, slabs)

    def hand(src, dst, sems, target):
        return pltpu.make_async_remote_copy(
            src_ref=src, dst_ref=dst, send_sem=sems[0], recv_sem=sems[1],
            device_id=(place, target), device_id_type=MESH)

    def down(turn, b):
        return hand(stage.at[0, b], halo.at[turn, 0, b], (halo_send.at[turn, 0, b], halo_recv.at[turn, 0, b]), after)

    def up(turn, b):
        return hand(stage.at[1, b], halo.at[turn, 1, b], (halo_send.at[turn, 1, b], halo_recv.at[turn, 1, b]), before)

    def down_rates():
        return hand(local, nearby.at[0], (near_send.at[0], near_recv.at[0]), after)

    def up_rates():
        return hand(local, nearby.at[1], (near_send.at[1], near_recv.at[1]), before)

    def send(turn, b):
        now = turn * HALO % 2
        for h in range(HALO):
            stage[0, b, h] = buf[now, rows + h, pl.ds(b * half, half)]
            stage[1, b, h] = buf[now, HALO + h, pl.ds(b * half, half)]

        @pl.when(me < slabs - 1)
        def _():
            down(turn, b).start()
            if turn == 0 and b == 0:
                down_rates().start()

        @pl.when(me > 0)
        def _():
            up(turn, b).start()
            if turn == 0 and b == 0:
                up_rates().start()

    def settle(turn, b):
        @pl.when(me > 0)
        def _():
            down(turn, b).wait_recv()
            up(turn, b).wait_send()
            if turn == 0 and b == 0:
                down_rates().wait_recv()
                up_rates().wait_send()

        @pl.when(me < slabs - 1)
        def _():
            up(turn, b).wait_recv()
            down(turn, b).wait_send()
            if turn == 0 and b == 0:
                up_rates().wait_recv()
                down_rates().wait_send()

    count = count_ref[0]
    chunk = 32
    lane = lax.broadcasted_iota(jnp.int32, (chunk, cols), 1)
    first, last = lane == 0, lane == cols - 1

    def update(step, r, read, rates, spans):
        later = (step + 1) % 2
        active = jnp.where(step < count, 1.0, 0.0)
        rate = rates[0] * active
        half_rate = 0.5 * rate
        force = rates[1] * active
        for c in spans:
            s = pl.ds(c, chunk)
            f = read(r, s)
            left = jnp.where(first, 0.0, pltpu.roll(f, 1, 1))
            right = jnp.where(last, 0.0, pltpu.roll(f, cols - 1, 1))
            lap = read(r + 1, s) + read(r - 1, s) + right + left - 4.0 * f
            th = jnp.tanh(f)
            buf[later, HALO + r, s] = f + (rate + half_rate * (th * th)) * lap + amp_ref[s] * force

    def edge(step, r, b):
        turn, i = step // HALO, step % HALO

        def read(at, s):
            inside = pl.ds(s.start - b * half, s.size)
            if i == 0 and at < 0:
                return halo[turn, 0, b, HALO + at, inside]
            if i == 0 and at >= rows:
                return halo[turn, 1, b, at - rows, inside]
            return buf[step % 2, HALO + at, s]

        if r < 0:
            rates = [nearby[0, n, rows + r : rows + r + 1] for n in range(2)]
        elif r >= rows:
            rates = [nearby[1, n, r - rows : r - rows + 1] for n in range(2)]
        else:
            rates = [local[n, r : r + 1] for n in range(2)]
        update(step, r, read, rates, range(b * half, (b + 1) * half, chunk))

    for b in range(BATCHES):
        send(0, b)
    for turn in range(STEPS // HALO):
        for i in range(HALO):
            step = turn * HALO + i

            def inner(r, carry):
                update(step, r, lambda at, s: buf[step % 2, HALO + at, s], [local[n, pl.ds(r, 1)] for n in range(2)],
                       range(0, snaps, chunk))
                return carry

            lax.fori_loop(1 + i, rows - 1 - i, inner, 0)
        for b in range(BATCHES):
            settle(turn, b)
            for i in range(HALO):
                step = turn * HALO + i
                for r in list(range(i + 1 - HALO, 1 + i)) + list(range(rows - 1 - i, rows + HALO - 1 - i)):
                    edge(step, r, b)
            if turn < STEPS // HALO - 1:
                send(turn + 1, b)

    end = STEPS % 2

    width = cols // places
    slot = lax.broadcasted_iota(jnp.int32, (chunk, cols), 1) // width

    def pack(i, carry):
        group = i // (snaps // chunk)
        s = pl.ds(pl.multiple_of(i % (snaps // chunk) * chunk, chunk), chunk)
        parts = [buf[end, HALO + group * places + j, s] for j in range(places)]
        for q in range(places):
            whole = parts[q]
            for j in range(places):
                if j != q:
                    whole = jnp.where(slot == j, pltpu.roll(parts[j], (j - q) % places * width, 1), whole)
            packed[q, group, s] = whole
        return carry

    lax.fori_loop(0, groups * (snaps // chunk), pack, 0)

    def beside(k, src, dst, sems):
        return pltpu.make_async_remote_copy(
            src_ref=src, dst_ref=dst, send_sem=sems[0].at[k], recv_sem=sems[1].at[k],
            device_id=(lax.rem(place + k, places), me), device_id_type=MESH)

    def along(k, src, dst, sems):
        return pltpu.make_async_remote_copy(
            src_ref=src, dst_ref=dst, send_sem=sems[0].at[k], recv_sem=sems[1].at[k],
            device_id=(place, lax.rem(me + k, slabs)), device_id_type=MESH)

    def swap(k):
        return beside(k, packed.at[lax.rem(place + k, places)], fields.at[place], (x_send, x_recv))

    for k in range(1, places):
        swap(k).start()

    def products(i, acc):
        pair = jnp.concatenate([buf[end, HALO + 2 * i], buf[end, HALO + 2 * i + 1]], axis=1)
        return acc + dot_t(pair, pair)

    part[...] = lax.fori_loop(0, rows // 2, products, jnp.zeros((snaps, snaps), jnp.float32))

    def scatter(k):
        peer = lax.rem(me + k, slabs)
        return along(k, part.at[pl.ds(peer * share, share)], pieces.at[k], (rs_send, rs_recv))

    def gather(k):
        return along(k, total, grams.at[place, pl.ds(me * share, share)], (ag_send, ag_recv))

    for k in range(1, slabs):
        scatter(k).start()
    for group in range(groups):
        fields[place, group] = packed[place, group]
    acc = part[pl.ds(pl.multiple_of(me * share, 8), share)]
    for k in range(1, slabs):
        scatter(k).wait_recv()
        acc = acc + pieces[k]
    total[...] = acc
    for k in range(1, slabs):
        gather(k).start()
    grams[place, pl.ds(pl.multiple_of(me * share, 8), share)] = acc
    for k in range(1, slabs):
        gather(k).wait_recv()

    def lend(k):
        return beside(k, grams.at[place], grams.at[place], (g_send, g_recv))

    def share_mix(k):
        return beside(k, mixes.at[place], mixes.at[place], (m_send, m_recv))

    for k in range(1, places):
        lend(k).start()
    mixes[place] = mixings([grams[place]], omega_rows(signs_ref[0]), [out0])[0]
    for k in range(1, places):
        share_mix(k).start()
    for k in range(1, places):
        swap(k).wait_recv()
    for k in range(1, places):
        share_mix(k).wait_recv()
    for i in range(places):
        for group in range(groups):
            every_ref[i, group] = dot(mixes[i], fields[i, group])

    def piece(i):
        return jnp.concatenate([every_ref[i, g] for g in range(groups)], axis=1)

    def stacked(i):
        return jnp.concatenate([piece(2 * i), piece(2 * i + 1)], axis=0)

    at = 0
    for i in range(count_pairs):
        for j in range(i + 1, count_pairs):
            tall[at : at + 2 * modes] = dot_t(stacked(i), stacked(j))
            at += 2 * modes
    for i in range(0, count_pairs, 2):
        tall[at : at + modes] = jnp.concatenate(
            [dot_t(piece(2 * h), piece(2 * h + 1)) for h in (i, i + 1)], axis=1)
        at += modes
    span = at // slabs

    def scatter_tall(k):
        peer = lax.rem(me + k, slabs)
        return along(k, tall.at[pl.ds(peer * span, span)], bits.at[k], (rt_send, rt_recv))

    def across(k):
        return beside(k, extra.at[place], extra.at[place], (px_send, px_recv))

    def gather_tall(k):
        return along(k, mine, cross_ref.at[pl.ds(me * span, span)], (at_send, at_recv))

    for k in range(1, slabs):
        scatter_tall(k).start()
    for k in range(1, places):
        lend(k).wait_recv()
    for i in range(places):
        own_ref[i] = dot_t(dot(mixes[i], grams[i]), mixes[i])
    acc = tall[pl.ds(pl.multiple_of(me * span, 8), span)]
    for k in range(1, slabs):
        scatter_tall(k).wait_recv()
        acc = acc + bits[k]
    extra[place] = acc
    for k in range(1, places):
        across(k).start()
    for k in range(1, places):
        across(k).wait_recv()
    acc = extra[0]
    for k in range(1, places):
        acc = acc + extra[k]
    mine[...] = acc
    for k in range(1, slabs):
        gather_tall(k).start()
    cross_ref[pl.ds(pl.multiple_of(me * span, 8), span)] = acc
    for k in range(1, slabs):
        scatter(k).wait_send()
        gather(k).wait_send()
        scatter_tall(k).wait_send()
    for k in range(1, places):
        swap(k).wait_send()
        lend(k).wait_send()
        share_mix(k).wait_send()
        across(k).wait_send()
    for k in range(1, slabs):
        gather_tall(k).wait()
    merge_levels(every_ref, own_ref, cross_ref, signs_ref, modes_ref, out0, out1)

def flow(slabs, places, x, coef, source, table, idx, count, omega_t):
    rows, cols = coef.shape
    snaps = x.shape[0] // rows
    modes = omega_t.shape[1]
    groups = rows // places
    pairs = places // 2
    high = pairs * (pairs - 1) // 2 * 2 * modes + pairs // 2 * modes
    f32 = jnp.float32

    def sems(*shape):
        return [pltpu.SemaphoreType.DMA(shape)] * 2

    inner = [(places, groups, modes, cols), (places, modes, modes), (high, 2 * modes)]
    return pl.pallas_call(
        functools.partial(flow_kernel, slabs, places),
        out_shape=jax.ShapeDtypeStruct((rows, cols // places, modes), f32),
        in_specs=[HBM, HBM, HBM, HBM, HBM, SMEM, HBM],
        out_specs=VMEM,
        scratch_shapes=[pltpu.VMEM(shape, f32) for shape in inner] + [
            pltpu.VMEM(x.shape, f32),
            pltpu.VMEM(table.shape, f32),
            pltpu.VMEM(idx.shape, jnp.int32),
            pltpu.VMEM(omega_t.shape, jnp.int32),
            pltpu.SemaphoreType.DMA((6,)),
            pltpu.VMEM((2, rows + 2 * HALO, snaps, cols), f32),
            pltpu.VMEM((STEPS // HALO, 2, BATCHES, HALO, snaps // BATCHES, cols), f32),
            pltpu.VMEM((2, BATCHES, HALO, snaps // BATCHES, cols), f32),
            pltpu.VMEM((2, rows, cols), f32),
            pltpu.VMEM((2, 2, rows, cols), f32),
            pltpu.VMEM((snaps, cols), f32),
            pltpu.VMEM((snaps, snaps), f32),
            pltpu.VMEM((slabs, snaps // slabs, snaps), f32),
            pltpu.VMEM((snaps // slabs, snaps), f32),
            pltpu.VMEM((places, groups, snaps, cols), f32),
            pltpu.VMEM((places, groups, snaps, cols), f32),
            pltpu.VMEM((places, snaps, snaps), f32),
            pltpu.VMEM((places, modes, snaps), f32),
            pltpu.VMEM((high, 2 * modes), f32),
            pltpu.VMEM((slabs, high // slabs, 2 * modes), f32),
            pltpu.VMEM((high // slabs, 2 * modes), f32),
            pltpu.VMEM((places, high // slabs, 2 * modes), f32),
            pltpu.VMEM((modes, 128), f32),
            pltpu.VMEM((modes, 128), f32),
        ] + sems(2) + sems(STEPS // HALO, 2, BATCHES) + 2 * sems(slabs) + 3 * sems(places)
        + sems(slabs) + sems(places) + sems(slabs),
        compiler_params=pltpu.CompilerParams(collective_id=0, has_side_effects=True, vmem_limit_bytes=VMEM_LIMIT),
    )(x, coef, source, table, idx, count, omega_t)


def eliminate(problems, outs):
    size = problems[0][0].shape[0]
    blocks = size // 8
    wide = 128
    sub = lax.broadcasted_iota(jnp.int32, (8, wide), 0)

    def split(value):
        return tuple(value[8 * b : 8 * b + 8] for b in range(blocks))

    def padded(m):
        return jnp.concatenate([m, jnp.zeros((size, wide - size), jnp.float32)], axis=1)

    start = tuple((split(padded(m)), split(r)) for m, r in problems)

    def spread(value, k):
        return jnp.broadcast_to(value[k : k + 1], (8, wide))

    def body(t, carry):
        states = []
        for ms, rs in carry:
            cols = [jnp.broadcast_to(ms[0][:, k : k + 1], (8, wide)) for k in range(8)]
            zero = jnp.zeros((8, wide), jnp.float32)
            states.append([ms[0], rs[0], cols, zero, zero, spread(cols[0], 0)])
        for k in range(8):
            for state in states:
                m0, r0, cols, done, scale, pivot = state
                inv = 1.0 / pivot
                done = jnp.where(sub == k, r0 * lax.rsqrt(pivot), done)
                scale = jnp.where(sub == k, inv, scale)
                hidden = jnp.where(sub == k, 0.0, cols[k])
                heads = [spread(c, k) if j > k else None for j, c in enumerate(cols)]
                if k < 7:
                    pivot = spread(cols[k + 1], k + 1) - spread(cols[k], k + 1) * heads[k + 1] * inv
                cols = [c if j <= k else c - hidden * heads[j] * inv for j, c in enumerate(cols)]
                m0 = m0 - hidden * spread(m0, k) * inv
                r0 = r0 - hidden * spread(r0, k) * inv
                state[:] = [m0, r0, cols, done, scale, pivot]
        following = []
        for (ms, rs), (m0, r0, _, done, scale, _), out in zip(carry, states, outs):
            out[pl.ds(pl.multiple_of(8 * t, 8), 8), :] = done
            rows_m = [spread(m0 * scale, k) for k in range(8)]
            rows_r = [spread(r0 * scale, k) for k in range(8)]
            next_m, next_r = [], []
            for m, r in zip(ms[1:], rs[1:]):
                less_m = less_r = 0.0
                for k in range(8):
                    col = jnp.broadcast_to(m[:, k : k + 1], (8, wide))
                    less_m, less_r = less_m + col * rows_m[k], less_r + col * rows_r[k]
                next_m.append(pltpu.roll(m - less_m, wide - 8, 1))
                next_r.append(r - less_r)
            zero = jnp.zeros((8, wide), jnp.float32)
            following.append((tuple(next_m + [zero]), tuple(next_r + [zero])))
        return tuple(following)

    lax.fori_loop(0, blocks, body, start)


def omega_rows(signs):
    return (2.0 * signs.astype(jnp.float32) - 1.0) / math.sqrt(signs.shape[1])


def shifted(m):
    size = m.shape[0]
    eye = lax.broadcasted_iota(jnp.int32, m.shape, 0) == lax.broadcasted_iota(jnp.int32, m.shape, 1)
    trace = jnp.sum(jnp.where(eye, m, 0.0), keepdims=True)
    return m + jnp.where(eye, (0.0001 / size) * trace, 0.0)


def mixings(grams, omega_t, outs):
    size = omega_t.shape[0]
    moments = [shifted(dot_t(dot(omega_t, g), omega_t)) for g in grams]
    eliminate([(m, omega_t) for m in moments], outs)
    lefts = [out[...] for out in outs[: len(grams)]]
    inners = []
    for left, g in zip(lefts, grams):
        hmat = dot(left, g)
        inners.append(shifted(dot_t(hmat, hmat)))
    pad = jnp.zeros((size, 128 - size), jnp.float32)
    eliminate([(c, jnp.concatenate([c, pad], axis=1)) for c in inners], outs)
    return [dot(out[:, :size], left) for out, left in zip(outs, lefts)]


def merge_levels(every_ref, own_ref, cross_ref, omega_ref, modes_ref, *outs):
    places, groups, modes, cols = every_ref.shape
    size = 2 * modes
    width = cols // places
    count = places // 2
    blocks = {}
    at = 0
    for i in range(count):
        for j in range(i + 1, count):
            blocks[i, j] = cross_ref[at : at + size]
            at += size
    for i in range(0, count, 2):
        both = cross_ref[at : at + modes]
        at += modes
        for h in range(2):
            inner = both[:, h * modes : (h + 1) * modes]
            top = jnp.concatenate([own_ref[2 * (i + h)], inner], axis=1)
            bottom = jnp.concatenate([jnp.transpose(inner), own_ref[2 * (i + h) + 1]], axis=1)
            blocks[i + h, i + h] = jnp.concatenate([top, bottom], axis=0)
    trees = None
    level = 0
    while count:
        mixes = []
        for at in range(0, count, 2):
            some = range(at, min(at + 2, count))
            mixes += mixings([0.5 * blocks[i, i] for i in some], omega_rows(omega_ref[level + 1]), outs)
        mixes = [0.5**0.5 * m for m in mixes]
        if trees is None:
            trees = mixes
        else:
            trees = [
                jnp.concatenate([dot(m[:, :modes], trees[2 * i]), dot(m[:, modes:], trees[2 * i + 1])], axis=1)
                for i, m in enumerate(mixes)
            ]
        count //= 2
        level += 1
        if count:
            fine = {}
            for i in range(2 * count):
                for j in range(i, 2 * count):
                    fine[i, j] = dot_t(dot(mixes[i], blocks[i, j]), mixes[j])
            blocks = {}
            for i in range(count):
                for j in range(i, count):
                    lower = fine[2 * i + 1, 2 * j] if i < j else jnp.transpose(fine[2 * i, 2 * j + 1])
                    top = jnp.concatenate([fine[2 * i, 2 * j], fine[2 * i, 2 * j + 1]], axis=1)
                    bottom = jnp.concatenate([lower, fine[2 * i + 1, 2 * j + 1]], axis=1)
                    blocks[i, j] = jnp.concatenate([top, bottom], axis=0)
    tree = trees[0]
    for group in range(groups):
        stacked = jnp.concatenate([every_ref[i, group] for i in range(places)], axis=0)
        whole = jnp.transpose(dot(tree, stacked))
        for j in range(places):
            modes_ref[group * places + j] = whole[j * width : (j + 1) * width]


def per_device(slabs, places, init_state, coef, source, amplitudes, sample_idx, step_counts, sketch_signs):
    _, snaps, rows, cols = init_state.shape
    signs = jnp.swapaxes(sketch_signs, 1, 2)
    out = flow(slabs, places, init_state.reshape(snaps * rows, cols), coef[0], source,
               amplitudes.reshape(1, -1), sample_idx, step_counts, signs)
    return jnp.transpose(out, (2, 0, 1))


def solution(mesh):
    return jax.shard_map(
        functools.partial(per_device, mesh.shape["slab"], mesh.shape["param"]),
        mesh=mesh,
        in_specs=(
            P("param", None, "slab", None),
            P("param", "slab", None),
            P("slab", None),
            P(),
            P("param", None),
            P("param"),
            P(),
        ),
        out_specs=P(None, "slab", "param"),
        check_vma=False,
    )
```
